128 devices in a mesh: drop: 8 (over x, core), blk: 16 (over z, y).
Axes of the slice: x: 4, y: 4, z: 4, core: 2. Of those that a mesh axis runs over, the one named last changes fastest.
Arguments:
- right_side: float32 [65536, 128], P(('drop', 'blk')), may hold values from -6 to 6
- near_blocks: bfloat16 [512, 40, 128, 128], P(('drop', 'blk')), may hold values from -0.15625 to 0.15625
- neighbours: int32 [512, 40], P(('drop', 'blk')), may hold values from 0 to 191
- counts: int32 [512], P(('drop', 'blk')), may hold values from 1 to 40
- leaf_inverse: bfloat16 [512, 128, 128], P(('drop', 'blk'))
- couple_left: bfloat16 [3, 64, 65536], P(None, None, ('drop', 'blk')), may hold values from -0.75 to 0.75
- couple_right: bfloat16 [3, 64, 65536], P(None, None, ('drop', 'blk')), may hold values from -0.0625 to 0.0625
- prec_left: bfloat16 [3, 64, 65536], P(None, None, ('drop', 'blk')), may hold values from -1 to 1
- prec_right: bfloat16 [3, 64, 65536], P(None, None, ('drop', 'blk')), may hold values from -0.0625 to 0.0625
Outputs:
- solution: float32 [65536, 128], P(('drop', 'blk'))
- residual: float32 [65536, 128], P(('drop', 'blk'))
The draws below stay inside these ranges and needn't reach their ends.
Inputs may be any that keep to these rules, and one draw needn't show every extreme that they name: `neighbours`: the three groups' blocks are numbered group g - 1 first, each group's blocks in row order. Slots k >= counts of a row are ignored.
All inputs are finite; a program needn't handle non-finite values.
Results may differ from the reference program's by a relative error of at most 0.035.
Values may be sent and summed in bfloat16 or wider, within the bound.
No kernel may reach another device: no remote copies, remote signals or barrier semaphores. Data moves between devices by JAX's collectives and lax.ppermute only.
A program may use at most 64 MiB of HBM per device.

```python
import jax
import jax.numpy as jnp
from jax import lax

BS = 128
R = 64
NBD = 4
NRHS = 128
K = 40
LEVELS = 3
ITERS = 3
NBLK = 512
ROWS = 65536
WIN = 192
N_DROP = 8
N_BLK = 16


def draw_leaf_inverse(key, part):
    key = jax.random.fold_in(key, 7)
    noise = jax.random.normal(key, (NBLK, BS, BS), jnp.float32)
    diagonal = jnp.eye(BS, dtype=jnp.float32)
    return (0.6 * diagonal[None] + 0.25 * BS ** (-0.5) * noise).astype(jnp.bfloat16)


def plant(drawn, own_key, least, largest):
    dims = drawn.shape
    spot = [jax.random.randint(jax.random.fold_in(own_key, axis), (), 0, dims[axis]) for axis in range(len(dims))]
    drawn = drawn.at[tuple(spot)].set(least)
    longest = dims.index(max(dims))
    spot[longest] = (spot[longest] + 1) % dims[longest]
    return drawn.at[tuple(spot)].set(largest)


def block_levels(key, dims, split, least, high):
    factor_of = 1.0
    for axis_at, shards_of in split:
        steps = jax.random.uniform(jax.random.fold_in(jax.random.fold_in(key, 6), axis_at), (shards_of,), jnp.float32, least / len(split), high / len(split))
        factor_of = factor_of * jnp.repeat(jnp.exp(steps), dims[axis_at] // shards_of).reshape((-1,) + (1,) * (len(dims) - 1 - axis_at))
    return factor_of


def normal_values(rng, dims, scale, limit, split=(), held_as=jnp.bfloat16):
    drawn = jax.random.normal(rng, dims, jnp.float32) * scale
    if len(split) > 0:
        drawn = block_levels(rng, dims, split, -0.22, 0.18) * drawn
    return jnp.clip(drawn, min=-limit, max=limit).astype(held_as)


def setup_inputs(seed: int = 0) -> dict:
    splits = jax.random.split(jax.random.key(seed), 10)
    right_side = normal_values(splits[0], (ROWS, NRHS), 1.0, 6.0, ((0, 128),), jnp.float32)
    near_blocks = normal_values(splits[1], (NBLK, K, BS, BS), (0.7 * (BS * K) ** -0.5), 0.15625, ((0, 128),))
    neighbours = plant(jax.random.randint(splits[2], (NBLK, K), 0, WIN), jax.random.fold_in(splits[2], 1), 0, WIN - 1).astype(jnp.int32)
    counts = plant(jax.random.randint(splits[3], (NBLK,), 1, K + 1), jax.random.fold_in(splits[3], 1), 1, K).astype(jnp.int32)
    leaf_inverse = draw_leaf_inverse(jax.random.fold_in(splits[9], 71), 0)
    couple_left = normal_values(splits[5], (LEVELS, R, ROWS), R ** -0.5, 0.75, ((2, 128),))
    couple_right = normal_values(splits[6], (LEVELS, R, ROWS), (N_BLK * NBD * BS) ** -0.5, 0.0625, ((2, 128),))
    prec_left = normal_values(splits[7], (LEVELS, R, ROWS), (0.5 * R ** -0.5), 1.0, ((2, 128),))
    prec_right = normal_values(splits[8], (LEVELS, R, ROWS), (N_BLK * NBD * BS) ** -0.5, 0.0625, ((2, 128),))
    return dict(right_side=right_side, near_blocks=near_blocks, neighbours=neighbours, counts=counts, leaf_inverse=leaf_inverse, couple_left=couple_left, couple_right=couple_right, prec_left=prec_left, prec_right=prec_right)


def near_field(flat_b, near_blocks, neighbours, counts):
    group_blocks = N_BLK * NBD
    blocks = flat_b.reshape(N_DROP, group_blocks, BS, NRHS)
    zero = jnp.zeros((1, group_blocks, BS, NRHS), flat_b.dtype)
    padded = jnp.concatenate([zero, blocks, zero], 0)
    devices = N_DROP * N_BLK
    near_dev = near_blocks.reshape(devices, NBD, K, BS, BS)
    nbr_dev = neighbours.reshape(devices, NBD, K)
    cnt_dev = counts.reshape(devices, NBD)

    def one_device(args):
        device, nblk, nbr, cnt = args
        group = (device // N_BLK).astype(jnp.int32)
        window = lax.dynamic_slice_in_dim(padded, group, 3, 0).reshape(3 * group_blocks, BS, NRHS)
        picked = window[nbr]
        live = jnp.arange(K, dtype=jnp.int32)[None, :] < cnt[:, None]
        picked = jnp.where(live[:, :, None, None], picked, jnp.zeros((), picked.dtype))
        return jnp.einsum("bkij,bkjn->bin", nblk.astype(jnp.float32), picked.astype(jnp.float32))

    out = lax.map(one_device, (jnp.arange(devices, dtype=jnp.int32), near_dev, nbr_dev, cnt_dev))
    return out.reshape(ROWS, NRHS)


def coupling(flat_b, left, right, level):
    clusters = N_DROP >> level
    rows = ROWS // clusters
    field = flat_b.reshape(clusters, rows, NRHS).astype(jnp.float32)
    rfac = right.reshape(R, clusters, rows).astype(jnp.float32)
    term = jnp.einsum("kcr,crn->ckn", rfac, field)
    sib = term.reshape(clusters // 2, 2, R, NRHS)[:, ::-1].reshape(clusters, R, NRHS)
    sib = lax.optimization_barrier(sib.astype(jnp.bfloat16)).astype(jnp.float32)
    lfac = left.reshape(R, clusters, rows).astype(jnp.float32)
    return jnp.einsum("kcr,ckn->crn", lfac, sib).reshape(ROWS, NRHS)


def operate(solution, near_blocks, neighbours, counts, couple_left, couple_right):
    flat_b = solution.astype(jnp.bfloat16)
    image = solution + near_field(flat_b, near_blocks, neighbours, counts)
    for level in range(LEVELS):
        image = image + coupling(flat_b, couple_left[level], couple_right[level], level)
    return image


def precondition(resid, leaf_inverse, prec_left, prec_right):
    tiles = resid.astype(jnp.bfloat16).reshape(NBLK, BS, NRHS).astype(jnp.float32)
    fixed = jnp.einsum("bij,bjn->bin", leaf_inverse.astype(jnp.float32), tiles).reshape(ROWS, NRHS)
    for level in range(LEVELS):
        fixed = fixed - coupling(fixed.astype(jnp.bfloat16), prec_left[level], prec_right[level], level)
    return fixed


def reference(right_side, near_blocks, neighbours, counts, leaf_inverse, couple_left, couple_right, prec_left, prec_right):
    solution = precondition(right_side, leaf_inverse, prec_left, prec_right)
    resid = right_side
    for step in range(ITERS):
        resid = right_side - operate(solution, near_blocks, neighbours, counts, couple_left, couple_right)
        solution = solution + precondition(resid, leaf_inverse, prec_left, prec_right)
    return solution, resid
```

```python
import jax
import jax.numpy as jnp
from jax import lax
from jax.experimental import pallas as pl
from jax.experimental.pallas import tpu as pltpu
from jax.sharding import PartitionSpec as P

ITERS = 3
AXES = ("drop", "blk")
BS = 128
NBD = 4
SLOTS = 40
R = 64
ROWS = NBD * BS
RING = 4 * ROWS
TERMS = 3 * R
PIECE = RING + TERMS
BF = jnp.bfloat16
F32 = jnp.float32


def coords(i):
    return i // 32, i // 16 % 2, i % 4, i // 4 % 4


def index(x, core, y, z):
    return (x % 4) * 32 + core * 16 + (z % 4) * 4 + y % 4


def pull(source):
    return [(source(i), i) for i in range(128)]


def along(axis, other):
    def source(i):
        x, core, y, z = coords(i)
        even = (x + core) % 2 == 1
        if even == (axis == 1):
            return index(x, core, other(y), z)
        return index(x, core, y, other(z))

    return pull(source)


UP, DOWN = along(1, lambda d: d + 1), along(1, lambda d: d - 1)
FIRST_NEAR, FIRST_FAR = along(1, lambda d: d ^ 1), along(1, lambda d: 3 - d)
SECOND_NEAR, SECOND_FAR = along(2, lambda d: d ^ 1), along(2, lambda d: 3 - d)
CORE = pull(lambda i: i ^ 16)
CHIP_NEAR = pull(lambda i: i ^ 32)
CHIP_FAR = pull(lambda i: i ^ 96)


def groups_of_eight():
    out = []
    for p in range(4):
        for k in range(4):
            members = []
            for x, core in ((p, 1), (p + 1, 0)):
                for j in range(4):
                    members.append(index(x, core, k, j) if p % 2 == 0 else index(x, core, j, k))
            out.append(members)
    return out


EIGHTS = groups_of_eight()


def move(array, pairs):
    return lax.ppermute(array, AXES, pairs)


def ring(array):
    half = array.shape[0] // 2
    up, down = move(array, UP), move(array, DOWN)
    far_a, far_b = move(up[:half], UP), move(down[half:], DOWN)
    return [up, down, far_a, far_b]


def add_pairwise(term, steps):
    for pairs in steps:
        term = term + move(term.astype(BF), pairs).astype(F32)
    return term


def siblings(term):
    other = move(term.astype(BF), CORE)
    chip = term[R:] + other[R:].astype(F32)
    near = move(chip.astype(BF), CHIP_NEAR)
    half = chip[R:] + near[R:].astype(F32)
    far = move(half.astype(BF), CHIP_FAR)
    return jnp.concatenate([other[:R], near[:R], far], axis=0)


def dot(a, b):
    return jnp.dot(a.astype(BF), b.astype(BF), preferred_element_type=F32)


def dot_t(a, b):
    return lax.dot_general(
        a.astype(BF), b.astype(BF), (((0,), (0,)), ((), ())), preferred_element_type=F32
    )


def dot_bt(a, b):
    return lax.dot_general(
        a.astype(BF), b.astype(BF), (((1,), (1,)), ((), ())), preferred_element_type=F32
    )


def slot_tables(neighbours, counts):
    drop, blk = lax.axis_index("drop"), lax.axis_index("blk")
    core, mine = drop % 2, (blk % 4, blk // 4)
    kind = neighbours // 64
    group = drop - 1 + kind
    block = neighbours % 64
    owner, part = block // 4, block % 4
    place = lax.rem(kind - core + 3, 3)
    even = (drop // 2 + core) % 2 == 1
    y_first = even == (place < 2)
    y, z = owner % 4, owner // 4
    first = jnp.where(y_first, y, z)
    second = jnp.where(y_first, z, y)
    mine_first = jnp.where(y_first, mine[0], mine[1])
    apart = (first - mine_first + 4) % 4
    at = jnp.where(apart < 2, apart, 5 - apart)
    member = jnp.where(place == 1, 4, 0) + second
    row = member * PIECE + at * ROWS + part * BS
    slot = lax.broadcasted_iota(jnp.int32, neighbours.shape, 1)
    live = (slot < counts[:, None]) & (group >= 0) & (group <= 7)
    key = jnp.where(live, jnp.where(place < 2, 0, 1), 2)
    rank_key = key * SLOTS + slot
    rank = jnp.sum((rank_key[:, None, :] < rank_key[:, :, None]).astype(jnp.int32), axis=2)
    put = rank[:, :, None] == lax.broadcasted_iota(jnp.int32, (1, 1, SLOTS), 2)
    order = jnp.sum(jnp.where(put, slot[:, :, None], 0), axis=1)
    start = jnp.sum(jnp.where(put, row[:, :, None], 0), axis=1)
    n_pair = jnp.sum((key == 0).astype(jnp.int32), axis=1)
    n_live = jnp.sum((key < 2).astype(jnp.int32), axis=1)
    return order.reshape(-1), start.reshape(-1), n_pair, n_live


def near_kernel(order, start, n_pair, n_live, blocks, pair, other, out):
    q = pl.program_id(0)
    base = q * SLOTS

    def span(field, lo, hi, acc):
        def two(i, acc):
            j = lo + 2 * i
            k = jnp.minimum(j + 1, hi - 1)
            left = blocks[0, order[base + j]]
            right = blocks[0, order[base + k]]
            right = jnp.where(j + 1 < hi, right, jnp.zeros_like(right))
            upper = field[pl.ds(pl.multiple_of(start[base + j], 64), BS), :]
            lower = field[pl.ds(pl.multiple_of(start[base + k], 64), BS), :]
            return acc + jnp.dot(
                jnp.concatenate([left, right], axis=1),
                jnp.concatenate([upper, lower], axis=0),
                preferred_element_type=F32,
            )

        return lax.fori_loop(0, (hi - lo + 1) // 2, two, acc)

    acc = jnp.zeros((BS, BS), F32)
    acc = span(pair, 0, n_pair[q], acc)
    acc = span(other, n_pair[q], n_live[q], acc)
    out[...] = acc


def near(tables, near_blocks, pair, other):
    return pl.pallas_call(
        near_kernel,
        grid_spec=pltpu.PrefetchScalarGridSpec(
            num_scalar_prefetch=4,
            grid=(NBD,),
            in_specs=[
                pl.BlockSpec((1, SLOTS, BS, BS), lambda q, *_: (q, 0, 0, 0)),
                pl.BlockSpec((8 * PIECE, BS), lambda q, *_: (0, 0)),
                pl.BlockSpec((4 * PIECE, BS), lambda q, *_: (0, 0)),
            ],
            out_specs=pl.BlockSpec((BS, BS), lambda q, *_: (q, 0)),
        ),
        out_shape=jax.ShapeDtypeStruct((ROWS, BS), F32),
        compiler_params=pltpu.CompilerParams(vmem_limit_bytes=40 * 2**20),
        cost_estimate=pl.CostEstimate(flops=2 * 80 * BS**3, bytes_accessed=12 * 2**20, transcendentals=0),
    )(*tables, near_blocks, pair, other)


def leaf(resid, leaf_inverse):
    tiles = resid.astype(BF).reshape(NBD, BS, BS)
    return jnp.einsum("bij,bjn->bin", leaf_inverse, tiles, preferred_element_type=F32).reshape(ROWS, BS)


def first_siblings(z_ring, right, left):
    r0, r1, r2 = right[:, :R], right[:, R : 2 * R], right[:, 2 * R :]
    terms = dot_t(right, z_ring)
    cross = dot_t(right, left)
    low = jnp.concatenate([cross[R : 2 * R, :R], cross[2 * R :, :R]], axis=1)
    high = jnp.concatenate([cross[2 * R :, R : 2 * R]] * 2, axis=1)
    mine = add_pairwise(jnp.concatenate([terms, low, high], axis=0), (SECOND_NEAR, SECOND_FAR))
    other = move(mine.astype(BF), CORE).astype(F32)

    def parts(a):
        return a[:R], a[R : 2 * R], a[2 * R : 3 * R], a[3 * R : 4 * R, :R], a[3 * R : 4 * R, R:], a[4 * R :, :R]

    a0, a1, a2, m10, m20, m21 = parts(mine)
    b0, b1, b2, k10, k20, k21 = parts(other)
    t1 = a1 - dot(m10, b0) + b1 - dot(k10, a0)
    t2 = a2 - dot(m20, b0) + b2 - dot(k20, a0)
    m21 = m21 + k21
    chip = jnp.concatenate([t1, t2, jnp.concatenate([m21, m21], axis=1)], axis=0)
    near_chip = move(chip.astype(BF), CHIP_NEAR).astype(F32)
    s1, u2, k21 = near_chip[:R], near_chip[R : 2 * R], near_chip[2 * R :, :R]
    half = t2 - dot(m21, s1) + u2 - dot(k21, t1)
    s2 = move(half.astype(BF), CHIP_FAR)
    sums = jnp.concatenate([b0.astype(BF), s1.astype(BF), s2], axis=0)
    f1 = r1.astype(F32) - dot_bt(r0, k10)
    f2 = r2.astype(F32) - dot_bt(r0, k20) - dot_bt(f1, k21)
    folded = jnp.concatenate([r0, f1.astype(BF), f2.astype(BF)], axis=1)
    return sums, folded


def on_device(
    right_side, near_blocks, neighbours, counts, leaf_inverse, couple_left, couple_right, prec_left, prec_right
):
    upper = lax.axis_index("drop") % 2 == 0
    tables = slot_tables(neighbours, counts)

    def by_row(factors):
        return factors.reshape(TERMS, ROWS).T

    z = leaf(right_side, leaf_inverse)
    mine = jnp.concatenate([z.astype(BF), by_row(prec_right), by_row(prec_left), by_row(couple_right)], axis=1)
    whole = jnp.concatenate([mine] + ring(mine), axis=0)
    right, left, c_right = (whole[:, BS + i * TERMS : BS + (i + 1) * TERMS] for i in range(3))
    z_ring = whole[:, :BS]
    sums, folded = first_siblings(z_ring, right, left)
    c_left = couple_left.reshape(TERMS, ROWS)
    field = jnp.concatenate([z, z_ring[ROWS:].astype(F32)], axis=0) - dot(left, sums)

    for step in range(ITERS):
        field_b = field.astype(BF)
        c_terms = dot_t(c_right, field_b)
        piece = jnp.concatenate([field_b, c_terms.astype(BF)], axis=0)
        pieces = lax.all_to_all(
            jnp.broadcast_to(piece[None], (8, PIECE, BS)), AXES, 0, 0, tiled=True, axis_index_groups=EIGHTS
        )
        own = lax.dynamic_slice_in_dim(pieces, jnp.where(upper, 4, 0), 4, axis=0)
        other = move(own, CORE)
        c_sums = siblings(jnp.sum(own[:, RING:].astype(F32), axis=0))
        product = near(tables, near_blocks, pieces.reshape(8 * PIECE, BS), other.reshape(4 * PIECE, BS))
        x = field[:ROWS]
        resid = right_side - (x + product + dot_t(c_left, c_sums))
        z = leaf(resid, leaf_inverse)
        if step < ITERS - 1:
            rest = jnp.concatenate(ring(z.astype(BF)), axis=0)
            z_ring = jnp.concatenate([z, rest.astype(F32)], axis=0)
            terms = add_pairwise(dot_t(folded, z_ring), (SECOND_NEAR, SECOND_FAR))
            field = field + z_ring - dot(left, siblings(terms))
        else:
            terms = dot_t(folded[:ROWS], z)
            terms = add_pairwise(terms, (FIRST_NEAR, FIRST_FAR, SECOND_NEAR, SECOND_FAR))
            x = x + z - dot(left[:ROWS], siblings(terms))
    return x, resid


def solution(mesh):
    in_specs = (
        P(("drop", "blk"), None),
        P(("drop", "blk"), None, None, None),
        P(("drop", "blk"), None),
        P(("drop", "blk")),
        P(("drop", "blk"), None, None),
        P(None, None, ("drop", "blk")),
        P(None, None, ("drop", "blk")),
        P(None, None, ("drop", "blk")),
        P(None, None, ("drop", "blk")),
    )
    out_specs = (P(("drop", "blk"), None), P(("drop", "blk"), None))
    return jax.shard_map(on_device, mesh=mesh, in_specs=in_specs, out_specs=out_specs, check_vma=False)
```

```python
import jax
import jax.numpy as jnp
from jax import lax
from jax.experimental import pallas as pl
from jax.experimental.pallas import tpu as pltpu
from jax.sharding import PartitionSpec as P

ITERS = 3
AXES = ("drop", "blk")
BS = 128
NBD = 4
SLOTS = 40
R = 64
ROWS = NBD * BS
RING = 4 * ROWS
TERMS = 3 * R
PIECE = RING + TERMS
BF = jnp.bfloat16
F32 = jnp.float32


def coords(i):
    return i // 32, i // 16 % 2, i % 4, i // 4 % 4


def index(x, core, y, z):
    return (x % 4) * 32 + core * 16 + (z % 4) * 4 + y % 4


def pull(source):
    return [(source(i), i) for i in range(128)]


def along(axis, other):
    def source(i):
        x, core, y, z = coords(i)
        even = (x + core) % 2 == 1
        if even == (axis == 1):
            return index(x, core, other(y), z)
        return index(x, core, y, other(z))

    return pull(source)


FIRST = [along(1, lambda d, k=k: d + k) for k in (1, 3, 2)]
SECOND = [along(2, lambda d, k=k: d + k) for k in (1, 3, 2)]
CORE = pull(lambda i: i ^ 16)
CHIP = [pull(lambda i, k=k: i ^ (32 * k)) for k in (1, 2, 3)]


def groups_of_eight():
    out = []
    for p in range(4):
        for k in range(4):
            members = []
            for x, core in ((p, 1), (p + 1, 0)):
                for j in range(4):
                    members.append(index(x, core, k, j) if p % 2 == 0 else index(x, core, j, k))
            out.append(members)
    return out


EIGHTS = groups_of_eight()


def move(array, pairs):
    return lax.ppermute(array, AXES, pairs)


def ring(array):
    return [move(array, pairs) for pairs in FIRST]


def long_ring(array):
    half = array.shape[0] // 2
    up, down = move(array, FIRST[0]), move(array, FIRST[1])
    return [up, down, jnp.concatenate([move(up[:half], FIRST[0]), move(down[half:], FIRST[1])], axis=0)]


def add_over(term, steps):
    sent = term.astype(BF)
    return term + sum(move(sent, pairs).astype(F32) for pairs in steps)


def siblings(term):
    other = move(term.astype(BF), CORE)
    return siblings_of(other, term)


def siblings_of(other, term):
    chip = (term[R:] + other[R:].astype(F32)).astype(BF)
    near, far_a, far_b = move(chip[:R], CHIP[0]), move(chip[R:], CHIP[1]), move(chip[R:], CHIP[2])
    return jnp.concatenate([other[:R], near, (far_a.astype(F32) + far_b.astype(F32)).astype(BF)], axis=0)


def dot(a, b):
    return jnp.dot(a.astype(BF), b.astype(BF), preferred_element_type=F32)


def dot_t(a, b):
    return lax.dot_general(
        a.astype(BF), b.astype(BF), (((0,), (0,)), ((), ())), preferred_element_type=F32
    )


def dot_bt(a, b):
    return lax.dot_general(
        a.astype(BF), b.astype(BF), (((1,), (1,)), ((), ())), preferred_element_type=F32
    )


def slot_tables(neighbours, counts):
    drop, blk = lax.axis_index("drop"), lax.axis_index("blk")
    core, mine = drop % 2, (blk % 4, blk // 4)
    kind = neighbours // 64
    group = drop - 1 + kind
    block = neighbours % 64
    owner, part = block // 4, block % 4
    place = lax.rem(kind - core + 3, 3)
    even = (drop // 2 + core) % 2 == 1
    y_first = even == (place < 2)
    y, z = owner % 4, owner // 4
    first = jnp.where(y_first, y, z)
    second = jnp.where(y_first, z, y)
    mine_first = jnp.where(y_first, mine[0], mine[1])
    apart = (first - mine_first + 4) % 4
    at = jnp.where(apart < 2, apart, 5 - apart)
    member = jnp.where(place == 1, 4, 0) + second
    row = member * jnp.where(place < 2, PIECE, RING) + at * ROWS + part * BS
    slot = lax.broadcasted_iota(jnp.int32, neighbours.shape, 1)
    live = (slot < counts[:, None]) & (group >= 0) & (group <= 7)
    key = jnp.where(live, jnp.where(place < 2, 0, 1), 2)
    rank_key = key * SLOTS + slot
    rank = jnp.sum((rank_key[:, None, :] < rank_key[:, :, None]).astype(jnp.int32), axis=2)
    put = rank[:, :, None] == lax.broadcasted_iota(jnp.int32, (1, 1, SLOTS), 2)
    order = jnp.sum(jnp.where(put, slot[:, :, None], 0), axis=1)
    start = jnp.sum(jnp.where(put, row[:, :, None], 0), axis=1)
    n_pair = jnp.sum((key == 0).astype(jnp.int32), axis=1)
    n_live = jnp.sum((key < 2).astype(jnp.int32), axis=1)
    return order.reshape(-1), start.reshape(-1), n_pair, n_live


def near_kernel(order, start, lo, hi, blocks, field, before, out):
    for q in range(NBD):
        first, last = lo[q], hi[q]

        def two(i, acc, q=q, first=first, last=last):
            j = first + 2 * i
            k = jnp.minimum(j + 1, last - 1)
            left = blocks[q, order[q * SLOTS + j]]
            right = blocks[q, order[q * SLOTS + k]]
            right = jnp.where(j + 1 < last, right, jnp.zeros_like(right))
            upper = field[pl.ds(pl.multiple_of(start[q * SLOTS + j], 64), BS), :]
            lower = field[pl.ds(pl.multiple_of(start[q * SLOTS + k], 64), BS), :]
            return acc + jnp.dot(
                jnp.concatenate([left, right], axis=1),
                jnp.concatenate([upper, lower], axis=0),
                preferred_element_type=F32,
            )

        rows = pl.ds(q * BS, BS)
        out[rows, :] = lax.fori_loop(0, (last - first + 1) // 2, two, before[rows, :])


def near(order, start, lo, hi, near_blocks, field, before):
    small, whole = pl.BlockSpec(memory_space=pltpu.SMEM), pl.BlockSpec(memory_space=pltpu.VMEM)
    return pl.pallas_call(
        near_kernel,
        in_specs=[small] * 4 + [whole] * 3,
        out_specs=whole,
        out_shape=jax.ShapeDtypeStruct((ROWS, BS), F32),
        compiler_params=pltpu.CompilerParams(vmem_limit_bytes=32 * 2**20),
        cost_estimate=pl.CostEstimate(flops=2 * 80 * BS**3, bytes_accessed=10 * 2**20, transcendentals=0),
    )(order, start, lo, hi, near_blocks, field, before)


def leaf(resid, leaf_inverse):
    tiles = resid.astype(BF).reshape(NBD, BS, BS)
    return jnp.einsum("bij,bjn->bin", leaf_inverse, tiles, preferred_element_type=F32).reshape(ROWS, BS)


def first_terms(z, right, left):
    terms = dot(right, z)
    cross = dot_bt(right, left)
    low = jnp.concatenate([cross[R : 2 * R, :R], cross[2 * R :, :R]], axis=1)
    high = jnp.concatenate([cross[2 * R :, R : 2 * R]] * 2, axis=1)
    return jnp.concatenate([terms, low, high], axis=0)


def first_siblings(mine):
    other = move(mine.astype(BF), CORE).astype(F32)

    def parts(a):
        return a[:R], a[R : 2 * R], a[2 * R : 3 * R], a[3 * R : 4 * R, :R], a[3 * R : 4 * R, R:], a[4 * R :, :R]

    a0, a1, a2, m10, m20, m21 = parts(mine)
    b0, b1, b2, k10, k20, k21 = parts(other)
    t1 = a1 - dot(m10, b0) + b1 - dot(k10, a0)
    t2 = a2 - dot(m20, b0) + b2 - dot(k20, a0)
    m21 = m21 + k21
    chip = jnp.concatenate([t1, t2, jnp.concatenate([m21, m21], axis=1)], axis=0)
    near_chip = move(chip.astype(BF), CHIP[0]).astype(F32)
    s1, u2, k21 = near_chip[:R], near_chip[R : 2 * R], near_chip[2 * R :, :R]
    half = t2 - dot(m21, s1) + u2 - dot(k21, t1)
    s2 = move(half.astype(BF), CHIP[2])
    return jnp.concatenate([b0.astype(BF), s1.astype(BF), s2], axis=0), (k10, k20, k21)


def fold(right, mixes):
    k10, k20, k21 = mixes
    r0, r1, r2 = right[:R], right[R : 2 * R], right[2 * R :]
    f1 = r1.astype(F32) - dot(k10, r0)
    f2 = r2.astype(F32) - dot(k20, r0) - dot(k21, f1)
    return jnp.concatenate([r0, f1.astype(BF), f2.astype(BF)], axis=0)


def by_block(factors):
    return jnp.concatenate([factors[:, i * BS : (i + 1) * BS] for i in range(NBD)], axis=0)


def on_device(
    right_side, near_blocks, neighbours, counts, leaf_inverse, couple_left, couple_right, prec_left, prec_right
):
    upper = lax.axis_index("drop") % 2 == 0
    order, start, n_pair, n_live = slot_tables(neighbours, counts)
    none = jnp.zeros_like(n_pair)
    c_left, c_right, left, right = (
        f.reshape(TERMS, ROWS) for f in (couple_left, couple_right, prec_left, prec_right)
    )

    z = leaf(right_side, leaf_inverse)
    terms = first_terms(z, right, left)
    count = terms.shape[0]
    sent = jnp.concatenate([z.astype(BF), terms.astype(BF), by_block(left), by_block(c_right)], axis=0)
    rest = long_ring(sent)
    terms = terms + sum(a[ROWS : ROWS + count].astype(F32) for a in rest)
    sums, mixes = first_siblings(add_over(terms, SECOND))
    sums, order, start, n_pair, n_live = lax.optimization_barrier((sums, order, start, n_pair, n_live))
    at = ROWS + count
    ring_left = jnp.concatenate([a[at : at + NBD * TERMS] for a in [sent] + rest], axis=0).reshape(-1, TERMS, BS)
    at += NBD * TERMS
    ring_c = jnp.concatenate([a[at : at + NBD * TERMS] for a in [sent] + rest], axis=0).reshape(-1, TERMS, BS)
    ring_c = ring_c.transpose(1, 0, 2).reshape(TERMS, RING)

    def corrected(field, sums):
        fix = jnp.einsum("bkr,kn->brn", ring_left, sums, preferred_element_type=F32)
        return field - fix.reshape(RING, BS)

    field = corrected(jnp.concatenate([z] + [a[:ROWS].astype(F32) for a in rest], axis=0), sums)
    folded = fold(right, mixes)

    for step in range(ITERS):
        field_b = field.astype(BF)
        piece = jnp.concatenate([field_b, dot(ring_c, field_b).astype(BF)], axis=0)
        pieces = lax.all_to_all(
            jnp.broadcast_to(piece[None], (8, PIECE, BS)), AXES, 0, 0, tiled=True, axis_index_groups=EIGHTS
        )
        c_parts = lax.dynamic_slice(pieces, (jnp.where(upper, 4, 0), RING, 0), (4, TERMS, BS))
        c_terms = jnp.sum(c_parts.astype(F32), axis=0)
        c_other = move(c_terms.astype(BF), CORE)
        pieces, c_other = lax.optimization_barrier((pieces, c_other))
        own = lax.dynamic_slice(pieces, (jnp.where(upper, 4, 0), 0, 0), (4, RING, BS))
        other = move(own, CORE)
        c_sums = siblings_of(c_other, c_terms)
        x = field[:ROWS]
        image = near(order, start, none, n_pair, near_blocks, pieces.reshape(8 * PIECE, BS), x)
        image = near(order, start, n_pair, n_live, near_blocks, other.reshape(4 * RING, BS), image)
        resid = right_side - (image + dot_t(c_left, c_sums))
        z = leaf(resid, leaf_inverse)
        terms = dot(folded, z)
        if step < ITERS - 1:
            rest = ring(jnp.concatenate([z.astype(BF), terms.astype(BF)], axis=0))
            terms = terms + sum(a[ROWS:].astype(F32) for a in rest)
            sums = siblings(add_over(terms, SECOND))
            z_ring = jnp.concatenate([z] + [a[:ROWS].astype(F32) for a in rest], axis=0)
            field = corrected(field + z_ring, sums)
        else:
            sums = siblings(add_over(add_over(terms, FIRST), SECOND))
            x = x + z - dot_t(left, sums)
    return x, resid


def solution(mesh):
    in_specs = (
        P(("drop", "blk"), None),
        P(("drop", "blk"), None, None, None),
        P(("drop", "blk"), None),
        P(("drop", "blk")),
        P(("drop", "blk"), None, None),
        P(None, None, ("drop", "blk")),
        P(None, None, ("drop", "blk")),
        P(None, None, ("drop", "blk")),
        P(None, None, ("drop", "blk")),
    )
    out_specs = (P(("drop", "blk"), None), P(("drop", "blk"), None))
    return jax.shard_map(on_device, mesh=mesh, in_specs=in_specs, out_specs=out_specs, check_vma=False)
```

```python
import functools

import jax
import jax.numpy as jnp
from jax import lax
from jax.experimental import pallas as pl
from jax.experimental.pallas import tpu as pltpu
from jax.sharding import PartitionSpec as P

ITERS = 3
AXES = ("drop", "blk")
BS = 128
NBD = 4
SLOTS = 40
R = 64
ROWS = NBD * BS
RING = 4 * ROWS
TERMS = 3 * R
PIECE = RING + TERMS
BF = jnp.bfloat16
F32 = jnp.float32


def coords(i):
    return i // 32, i // 16 % 2, i % 4, i // 4 % 4


def index(x, core, y, z):
    return (x % 4) * 32 + core * 16 + (z % 4) * 4 + y % 4


def pull(source):
    return [(source(i), i) for i in range(128)]


def along(axis, other):
    def source(i):
        x, core, y, z = coords(i)
        even = (x + core) % 2 == 1
        if even == (axis == 1):
            return index(x, core, other(y), z)
        return index(x, core, y, other(z))

    return pull(source)


FIRST = [along(1, lambda d, k=k: d + k) for k in (1, 3, 2)]
SECOND = [along(2, lambda d, k=k: d + k) for k in (1, 3, 2)]
CORE = pull(lambda i: i ^ 16)
CHIP = [pull(lambda i, k=k: i ^ (32 * k)) for k in (1, 2, 3)]


def groups_of_eight():
    out = []
    for p in range(4):
        for k in range(4):
            members = []
            for x, core in ((p, 1), (p + 1, 0)):
                for j in range(4):
                    members.append(index(x, core, k, j) if p % 2 == 0 else index(x, core, j, k))
            out.append(members)
    return out


EIGHTS = groups_of_eight()


def move(array, pairs):
    return lax.ppermute(array, AXES, pairs)


def ring(array):
    return [move(array, pairs) for pairs in FIRST]


def long_ring(array):
    half = array.shape[0] // 2
    up, down = move(array, FIRST[0]), move(array, FIRST[1])
    return [up, down, jnp.concatenate([move(up[:half], FIRST[0]), move(down[half:], FIRST[1])], axis=0)]


def add_over(term, steps):
    sent = term.astype(BF)
    return term + sum(move(sent, pairs).astype(F32) for pairs in steps)


def siblings(term):
    other = move(term.astype(BF), CORE)
    chip = term[R:] + other[R:].astype(F32)
    near = move(chip.astype(BF), CHIP[0])
    half = chip[R:] + near[R:].astype(F32)
    far = move(half.astype(BF), CHIP[2])
    return jnp.concatenate([other[:R], near[:R], far], axis=0)


def siblings_beside(other, term):
    chip = (term[R:] + other[R:].astype(F32)).astype(BF)
    near, far_a, far_b = move(chip[:R], CHIP[0]), move(chip[R:], CHIP[1]), move(chip[R:], CHIP[2])
    return jnp.concatenate([other[:R], near, (far_a.astype(F32) + far_b.astype(F32)).astype(BF)], axis=0)


def dot(a, b):
    return jnp.dot(a.astype(BF), b.astype(BF), preferred_element_type=F32)


def dot_t(a, b):
    return lax.dot_general(
        a.astype(BF), b.astype(BF), (((0,), (0,)), ((), ())), preferred_element_type=F32
    )


def dot_bt(a, b):
    return lax.dot_general(
        a.astype(BF), b.astype(BF), (((1,), (1,)), ((), ())), preferred_element_type=F32
    )


def slot_tables(neighbours, counts, half):
    drop, blk = lax.axis_index("drop"), lax.axis_index("blk")
    core, mine = drop % 2, (blk % 4, blk // 4)
    kind = neighbours // 64
    group = drop - 1 + kind
    block = neighbours % 64
    owner, part = block // 4, block % 4
    place = lax.rem(4 * kind + half + 8, 12) // 4
    even = (drop // 2 + core) % 2 == 1
    y_first = even == (place < 2)
    y, z = owner % 4, owner // 4
    first = jnp.where(y_first, y, z)
    second = jnp.where(y_first, z, y)
    mine_first = jnp.where(y_first, mine[0], mine[1])
    apart = (first - mine_first + 4) % 4
    at = jnp.where(apart < 2, apart, 5 - apart)
    member = jnp.where(place == 1, 4, 0) + second
    row = member * jnp.where(place < 2, PIECE, RING) + at * ROWS + part * BS
    slot = lax.broadcasted_iota(jnp.int32, neighbours.shape, 1)
    live = (slot < counts[:, None]) & (group >= 0) & (group <= 7)
    key = jnp.where(live, jnp.where(place < 2, 0, 1), 2)
    rank_key = key * SLOTS + slot
    rank = jnp.sum((rank_key[:, None, :] < rank_key[:, :, None]).astype(jnp.int32), axis=2)
    put = rank[:, :, None] == lax.broadcasted_iota(jnp.int32, (1, 1, SLOTS), 2)
    order = jnp.sum(jnp.where(put, slot[:, :, None], 0), axis=1)
    start = jnp.sum(jnp.where(put, jnp.where(live, row, 0)[:, :, None], 0), axis=1)
    n_pair = jnp.sum((key == 0).astype(jnp.int32), axis=1)
    n_live = jnp.sum((key < 2).astype(jnp.int32), axis=1)
    return order.reshape(-1), start.reshape(-1), n_pair, n_live


def near_kernel(width, order, start, lo, hi, blocks, field, before, out):
    rows = range(NBD)
    longest = hi[0] - lo[0]
    for q in rows[1:]:
        longest = jnp.maximum(longest, hi[q] - lo[q])

    def some(i, sums):
        new = []
        for q in rows:
            left, right = [], []
            for u in range(width):
                j = lo[q] + width * i + u
                at = q * SLOTS + jnp.minimum(j, SLOTS - 1)
                block = blocks[q, order[at]]
                left.append(jnp.where(j < hi[q], block, jnp.zeros_like(block)))
                row = jnp.minimum(start[at], field.shape[0] - BS)
                right.append(field[pl.ds(pl.multiple_of(row, 64), BS), :])
            new.append(
                sums[q]
                + jnp.dot(
                    jnp.concatenate(left, axis=1), jnp.concatenate(right, axis=0), preferred_element_type=F32
                )
            )
        return tuple(new)

    sums = tuple(before[q * BS : (q + 1) * BS, :] for q in rows)
    sums = lax.fori_loop(0, (longest + width - 1) // width, some, sums)
    for q in rows:
        out[q * BS : (q + 1) * BS, :] = sums[q]


def near(width, order, start, lo, hi, near_blocks, field, before):
    small, whole = pl.BlockSpec(memory_space=pltpu.SMEM), pl.BlockSpec(memory_space=pltpu.VMEM)
    return pl.pallas_call(
        functools.partial(near_kernel, width),
        in_specs=[small] * 4 + [whole] * 3,
        out_specs=whole,
        out_shape=jax.ShapeDtypeStruct((ROWS, BS), F32),
        compiler_params=pltpu.CompilerParams(vmem_limit_bytes=12 * 2**20),
        cost_estimate=pl.CostEstimate(flops=2 * 80 * BS**3, bytes_accessed=10 * 2**20, transcendentals=0),
    )(order, start, lo, hi, near_blocks, field, before)


def leaf(resid, leaf_inverse):
    tiles = resid.astype(BF).reshape(NBD, BS, BS)
    return jnp.einsum("bij,bjn->bin", leaf_inverse, tiles, preferred_element_type=F32).reshape(ROWS, BS)


def first_terms(z, right, left):
    terms = dot(right, z)
    cross = dot_bt(right, left)
    low = jnp.concatenate([cross[R : 2 * R, :R], cross[2 * R :, :R]], axis=1)
    high = jnp.concatenate([cross[2 * R :, R : 2 * R]] * 2, axis=1)
    return jnp.concatenate([terms, low, high], axis=0)


def first_siblings(mine):
    other = move(mine.astype(BF), CORE).astype(F32)

    def parts(a):
        return a[:R], a[R : 2 * R], a[2 * R : 3 * R], a[3 * R : 4 * R, :R], a[3 * R : 4 * R, R:], a[4 * R :, :R]

    a0, a1, a2, m10, m20, m21 = parts(mine)
    b0, b1, b2, k10, k20, k21 = parts(other)
    t1 = a1 - dot(m10, b0) + b1 - dot(k10, a0)
    t2 = a2 - dot(m20, b0) + b2 - dot(k20, a0)
    m21 = m21 + k21
    chip = jnp.concatenate([t1, t2, jnp.concatenate([m21, m21], axis=1)], axis=0)
    near_chip = move(chip.astype(BF), CHIP[0]).astype(F32)
    s1, u2, k21 = near_chip[:R], near_chip[R : 2 * R], near_chip[2 * R :, :R]
    half = t2 - dot(m21, s1) + u2 - dot(k21, t1)
    s2 = move(half.astype(BF), CHIP[2])
    return jnp.concatenate([b0.astype(BF), s1.astype(BF), s2], axis=0), (k10, k20, k21)


def fold(terms, mixes):
    k10, k20, k21 = mixes
    t0, t1, t2 = terms[:R], terms[R : 2 * R], terms[2 * R :]
    t1 = t1 - dot(k10, t0)
    t2 = t2 - dot(k20, t0) - dot(k21, t1)
    return jnp.concatenate([t0, t1, t2], axis=0)


def on_device(
    right_side, near_blocks, neighbours, counts, leaf_inverse, couple_left, couple_right, prec_left, prec_right
):
    half = 4 - 4 * (lax.axis_index("drop") % 2)
    order, start, n_pair, n_live = slot_tables(neighbours, counts, half)
    none = jnp.zeros_like(n_pair)
    c_left, c_right, left, right = (
        f.reshape(TERMS, ROWS) for f in (couple_left, couple_right, prec_left, prec_right)
    )

    facts = jnp.concatenate([left, c_right], axis=0)
    facts = [facts] + long_ring(facts)
    z = leaf(right_side, leaf_inverse)
    terms = first_terms(z, right, left)
    rest = ring(jnp.concatenate([z, terms], axis=0).astype(BF))
    terms = terms + sum(a[ROWS:].astype(F32) for a in rest)
    sums, mixes = first_siblings(add_over(terms, SECOND))
    sums, order, start, n_pair, n_live = lax.optimization_barrier((sums, order, start, n_pair, n_live))
    ring_left, ring_c = [a[:TERMS] for a in facts], [a[TERMS:] for a in facts]

    def corrected(field, sums):
        return field - jnp.concatenate([dot_t(a, sums) for a in ring_left], axis=0)

    field = corrected(jnp.concatenate([z] + [a[:ROWS].astype(F32) for a in rest], axis=0), sums)

    for step in range(ITERS):
        field_b = field.astype(BF)
        c_terms = sum(dot(a, field_b[i * ROWS : (i + 1) * ROWS]) for i, a in enumerate(ring_c))
        piece = jnp.concatenate([field_b, c_terms.astype(BF)], axis=0)
        pieces = lax.all_to_all(
            jnp.broadcast_to(piece[None], (8, PIECE, BS)), AXES, 0, 0, tiled=True, axis_index_groups=EIGHTS
        )
        c_parts = lax.dynamic_slice(pieces, (half, RING, 0), (4, TERMS, BS), allow_negative_indices=False)
        c_terms = jnp.sum(c_parts.astype(F32), axis=0)
        c_other = move(c_terms.astype(BF), CORE)
        pieces, c_other = lax.optimization_barrier((pieces, c_other))
        own = lax.dynamic_slice(pieces, (half, 0, 0), (4, RING, BS), allow_negative_indices=False)
        other = move(own, CORE)
        c_sums = siblings_beside(c_other, c_terms)
        x = field[:ROWS]
        image = near(8, order, start, none, n_pair, near_blocks, pieces.reshape(8 * PIECE, BS), x)
        image = near(4, order, start, n_pair, n_live, near_blocks, other.reshape(4 * RING, BS), image)
        image, c_sums = lax.optimization_barrier((image, c_sums))
        resid = right_side - (image + dot_t(c_left, c_sums))
        z = leaf(resid, leaf_inverse)
        terms = fold(dot(right, z), mixes)
        if step < ITERS - 1:
            terms = add_over(terms, FIRST)
            rest = ring(z.astype(BF))
            sums = siblings(add_over(terms, SECOND))
            z_ring = jnp.concatenate([z] + [a.astype(F32) for a in rest], axis=0)
            field = corrected(field + z_ring, sums)
        else:
            sums = siblings(add_over(add_over(terms, FIRST), SECOND))
            x = x + z - dot_t(left, sums)
    return x, resid


def solution(mesh):
    in_specs = (
        P(("drop", "blk"), None),
        P(("drop", "blk"), None, None, None),
        P(("drop", "blk"), None),
        P(("drop", "blk")),
        P(("drop", "blk"), None, None),
        P(None, None, ("drop", "blk")),
        P(None, None, ("drop", "blk")),
        P(None, None, ("drop", "blk")),
        P(None, None, ("drop", "blk")),
    )
    out_specs = (P(("drop", "blk"), None), P(("drop", "blk"), None))
    return jax.shard_map(on_device, mesh=mesh, in_specs=in_specs, out_specs=out_specs, check_vma=False)
```

```python
import functools

import jax
import jax.numpy as jnp
from jax import lax
from jax.experimental import pallas as pl
from jax.experimental.pallas import tpu as pltpu
from jax.sharding import PartitionSpec as P

ITERS = 3
AXES = ("drop", "blk")
BS = 128
NBD = 4
SLOTS = 40
R = 64
ROWS = NBD * BS
RING = 4 * ROWS
TERMS = 3 * R
PIECE = RING + TERMS
BF = jnp.bfloat16
F32 = jnp.float32


def coords(i):
    return i // 32, i // 16 % 2, i % 4, i // 4 % 4


def index(x, core, y, z):
    return (x % 4) * 32 + core * 16 + (z % 4) * 4 + y % 4


def pull(source):
    return [(source(i), i) for i in range(128)]


def along(axis, other):
    def source(i):
        x, core, y, z = coords(i)
        even = (x + core) % 2 == 1
        if even == (axis == 1):
            return index(x, core, other(y), z)
        return index(x, core, y, other(z))

    return pull(source)


FIRST = [along(1, lambda d, k=k: d + k) for k in (1, 3, 2)]
SECOND = [along(2, lambda d, k=k: d + k) for k in (1, 3, 2)]
CORE = pull(lambda i: i ^ 16)
CHIP = [pull(lambda i, k=k: i ^ (32 * k)) for k in (1, 2, 3)]


def groups_of_eight():
    out = []
    for p in range(4):
        for k in range(4):
            members = []
            for x, core in ((p, 1), (p + 1, 0)):
                for j in range(4):
                    members.append(index(x, core, k, j) if p % 2 == 0 else index(x, core, j, k))
            out.append(members)
    return out


EIGHTS = groups_of_eight()


def move(array, pairs):
    return lax.ppermute(array, AXES, pairs)


def ring(array):
    return [move(array, pairs) for pairs in FIRST]


def long_ring(array):
    half = array.shape[0] // 2
    up, down = move(array, FIRST[0]), move(array, FIRST[1])
    return [up, down, jnp.concatenate([move(up[:half], FIRST[0]), move(down[half:], FIRST[1])], axis=0)]


def add_over(term, steps):
    sent = term.astype(BF)
    return term + sum(move(sent, pairs).astype(F32) for pairs in steps)


def siblings(term):
    other = move(term.astype(BF), CORE)
    chip = term[R:] + other[R:].astype(F32)
    near = move(chip.astype(BF), CHIP[0])
    half = chip[R:] + near[R:].astype(F32)
    return other, near, move(half.astype(BF), CHIP[2])


def siblings_beside(other, term):
    chip = (term[R:] + other[R:].astype(F32)).astype(BF)
    return other, move(chip[:R], CHIP[0]), move(chip[R:], CHIP[1]), move(chip[R:], CHIP[2])


def sibling_sums(other, near, *far):
    last = far[0][...].astype(F32)
    for part in far[1:]:
        last = last + part[...].astype(F32)
    return jnp.concatenate([other[:R], near[:R], last.astype(BF)], axis=0)


def dot(a, b):
    return jnp.dot(a.astype(BF), b.astype(BF), preferred_element_type=F32)


def dot_t(a, b):
    return lax.dot_general(
        a.astype(BF), b.astype(BF), (((0,), (0,)), ((), ())), preferred_element_type=F32
    )


def dot_bt(a, b):
    return lax.dot_general(
        a.astype(BF), b.astype(BF), (((1,), (1,)), ((), ())), preferred_element_type=F32
    )


def slot_tables(neighbours, counts, half):
    drop, blk = lax.axis_index("drop"), lax.axis_index("blk")
    core, mine = drop % 2, (blk % 4, blk // 4)
    kind = neighbours // 64
    group = drop - 1 + kind
    block = neighbours % 64
    owner, part = block // 4, block % 4
    place = lax.rem(4 * kind + half + 8, 12) // 4
    even = (drop // 2 + core) % 2 == 1
    y_first = even == (place < 2)
    y, z = owner % 4, owner // 4
    first = jnp.where(y_first, y, z)
    second = jnp.where(y_first, z, y)
    mine_first = jnp.where(y_first, mine[0], mine[1])
    apart = (first - mine_first + 4) % 4
    at = jnp.where(apart < 2, apart, 5 - apart)
    member = jnp.where(place == 1, 4, 0) + second
    row = member * jnp.where(place < 2, PIECE, RING) + at * ROWS + part * BS
    slot = lax.broadcasted_iota(jnp.int32, neighbours.shape, 1)
    live = (slot < counts[:, None]) & (group >= 0) & (group <= 7)
    key = jnp.where(live, jnp.where(place < 2, 0, 1), 2)
    rank_key = key * SLOTS + slot
    rank = jnp.sum((rank_key[:, None, :] < rank_key[:, :, None]).astype(jnp.int32), axis=2)
    put = rank[:, :, None] == lax.broadcasted_iota(jnp.int32, (1, 1, SLOTS), 2)
    order = jnp.sum(jnp.where(put, slot[:, :, None], 0), axis=1)
    start = jnp.sum(jnp.where(put, jnp.where(live, row, 0)[:, :, None], 0), axis=1)
    n_pair = jnp.sum((key == 0).astype(jnp.int32), axis=1)
    n_live = jnp.sum((key < 2).astype(jnp.int32), axis=1)
    return order.reshape(-1), start.reshape(-1), n_pair, n_live


def near_kernel(width, order, start, lo, hi, blocks, field, before, out):
    rows = range(NBD)
    longest = hi[0] - lo[0]
    for q in rows[1:]:
        longest = jnp.maximum(longest, hi[q] - lo[q])

    def some(i, sums):
        new = []
        for q in rows:
            left, right = [], []
            for u in range(width):
                j = lo[q] + width * i + u
                at = q * SLOTS + jnp.minimum(j, SLOTS - 1)
                block = blocks[q, order[at]]
                left.append(jnp.where(j < hi[q], block, jnp.zeros_like(block)))
                row = jnp.minimum(start[at], field.shape[0] - BS)
                right.append(field[pl.ds(pl.multiple_of(row, 64), BS), :])
            new.append(
                sums[q]
                + jnp.dot(
                    jnp.concatenate(left, axis=1), jnp.concatenate(right, axis=0), preferred_element_type=F32
                )
            )
        return tuple(new)

    sums = tuple(before[q * BS : (q + 1) * BS, :] for q in rows)
    sums = lax.fori_loop(0, (longest + width - 1) // width, some, sums)
    for q in rows:
        out[q * BS : (q + 1) * BS, :] = sums[q]


def near(width, order, start, lo, hi, near_blocks, field, before):
    small, whole = pl.BlockSpec(memory_space=pltpu.SMEM), pl.BlockSpec(memory_space=pltpu.VMEM)
    return pl.pallas_call(
        functools.partial(near_kernel, width),
        in_specs=[small] * 4 + [whole] * 3,
        out_specs=whole,
        out_shape=jax.ShapeDtypeStruct((ROWS, BS), F32),
        compiler_params=pltpu.CompilerParams(vmem_limit_bytes=12 * 2**20),
        cost_estimate=pl.CostEstimate(flops=2 * 80 * BS**3, bytes_accessed=10 * 2**20, transcendentals=0),
    )(order, start, lo, hi, near_blocks, field, before)


def kernel_call(body, shapes, cost, *given):
    whole = pl.BlockSpec(memory_space=pltpu.VMEM)
    return pl.pallas_call(
        body,
        in_specs=[whole] * len(given),
        out_specs=[whole] * len(shapes),
        out_shape=[jax.ShapeDtypeStruct(*shape) for shape in shapes],
        compiler_params=pltpu.CompilerParams(vmem_limit_bytes=16 * 2**20),
        cost_estimate=pl.CostEstimate(flops=cost * 10**6, bytes_accessed=2**20, transcendentals=0),
    )(*given)


def start_kernel(has_field, *refs):
    *given, field, pieces = refs
    before, given = (given[0], given[1:]) if has_field else (None, given)
    z, up, down, far, other, near, last, *facts = given
    facts = facts[:4]
    sums = sibling_sums(other, near, last)
    c_terms = jnp.zeros((TERMS, BS), F32)
    for i, (part, fact) in enumerate(zip((z, up, down, far), facts)):
        rows = slice(i * ROWS, (i + 1) * ROWS)
        new = part[...].astype(F32) - dot_t(fact[:TERMS, :], sums)
        if has_field:
            new = before[rows, :] + new
        field[rows, :] = new
        new = new.astype(BF)
        for m in range(8):
            pieces[m, rows, :] = new
        c_terms = c_terms + dot(fact[TERMS:, :], new)
    c_terms = c_terms.astype(BF)
    for m in range(8):
        pieces[m, RING:, :] = c_terms


def finish_kernel(image, right_side, other, near, far_a, far_b, c_left, leaf_inverse, right, k10, k20, k21, resid, z, terms):
    sums = sibling_sums(other, near, far_a, far_b)
    left_over = right_side[...] - (image[...] + dot_t(c_left[...], sums))
    resid[...] = left_over
    left_over = left_over.astype(BF)
    for q in range(NBD):
        rows = slice(q * BS, (q + 1) * BS)
        z[rows, :] = dot(leaf_inverse[q], left_over[rows, :])
    terms[...] = fold(dot(right[...], z[...]), (k10[...], k20[...], k21[...]))


def leaf(resid, leaf_inverse):
    tiles = resid.astype(BF).reshape(NBD, BS, BS)
    return jnp.einsum("bij,bjn->bin", leaf_inverse, tiles, preferred_element_type=F32).reshape(ROWS, BS)


def first_terms(z, right, left):
    terms = dot(right, z)
    cross = dot_bt(right, left)
    low = jnp.concatenate([cross[R : 2 * R, :R], cross[2 * R :, :R]], axis=1)
    high = jnp.concatenate([cross[2 * R :, R : 2 * R]] * 2, axis=1)
    return jnp.concatenate([terms, low, high], axis=0)


def first_siblings(mine):
    other = move(mine.astype(BF), CORE).astype(F32)

    def parts(a):
        return a[:R], a[R : 2 * R], a[2 * R : 3 * R], a[3 * R : 4 * R, :R], a[3 * R : 4 * R, R:], a[4 * R :, :R]

    a0, a1, a2, m10, m20, m21 = parts(mine)
    b0, b1, b2, k10, k20, k21 = parts(other)
    t1 = a1 - dot(m10, b0) + b1 - dot(k10, a0)
    t2 = a2 - dot(m20, b0) + b2 - dot(k20, a0)
    m21 = m21 + k21
    chip = jnp.concatenate([t1, t2, jnp.concatenate([m21, m21], axis=1)], axis=0)
    near_chip = move(chip.astype(BF), CHIP[0]).astype(F32)
    s1, u2, k21 = near_chip[:R], near_chip[R : 2 * R], near_chip[2 * R :, :R]
    half = t2 - dot(m21, s1) + u2 - dot(k21, t1)
    s2 = move(half.astype(BF), CHIP[2])
    return (b0.astype(BF), s1.astype(BF), s2), (k10.astype(BF), k20.astype(BF), k21.astype(BF))


def fold(terms, mixes):
    k10, k20, k21 = mixes
    t0, t1, t2 = terms[:R], terms[R : 2 * R], terms[2 * R :]
    t1 = t1 - dot(k10, t0)
    t2 = t2 - dot(k20, t0) - dot(k21, t1)
    return jnp.concatenate([t0, t1, t2], axis=0)


def on_device(
    right_side, near_blocks, neighbours, counts, leaf_inverse, couple_left, couple_right, prec_left, prec_right
):
    half = 4 - 4 * (lax.axis_index("drop") % 2)
    order, start, n_pair, n_live = slot_tables(neighbours, counts, half)
    none = jnp.zeros_like(n_pair)
    c_left, c_right, left, right = (
        f.reshape(TERMS, ROWS) for f in (couple_left, couple_right, prec_left, prec_right)
    )

    facts = jnp.concatenate([left, c_right], axis=0)
    facts = [facts] + long_ring(facts)
    z = leaf(right_side, leaf_inverse)
    terms = first_terms(z, right, left)
    rest = ring(jnp.concatenate([z, terms], axis=0).astype(BF))
    terms = terms + sum(a[ROWS:].astype(F32) for a in rest)
    sums, mixes = first_siblings(add_over(terms, SECOND))
    field = None
    z_ring = [z] + [a[:ROWS] for a in rest]
    field_shape, piece_shape = ((RING, BS), F32), ((8, PIECE, BS), BF)

    for step in range(ITERS):
        given = [*z_ring, *sums, *facts]
        given = given + [order, start, n_pair, n_live] if step == 0 else [field] + given
        field, pieces = kernel_call(
            functools.partial(start_kernel, step > 0), (field_shape, piece_shape), 500, *given
        )
        pieces = lax.all_to_all(pieces, AXES, 0, 0, tiled=True, axis_index_groups=EIGHTS)
        c_parts = lax.dynamic_slice(pieces, (half, RING, 0), (4, TERMS, BS), allow_negative_indices=False)
        c_terms = jnp.sum(c_parts.astype(F32), axis=0)
        c_other = move(c_terms.astype(BF), CORE)
        pieces, c_other = lax.optimization_barrier((pieces, c_other))
        own = lax.dynamic_slice(pieces, (half, 0, 0), (4, RING, BS), allow_negative_indices=False)
        other = move(own, CORE)
        c_sums = siblings_beside(c_other, c_terms)
        x = field[:ROWS]
        image = near(8, order, start, none, n_pair, near_blocks, pieces.reshape(8 * PIECE, BS), x)
        image = near(4, order, start, n_pair, n_live, near_blocks, other.reshape(4 * RING, BS), image)
        resid, z, terms = kernel_call(
            finish_kernel,
            (((ROWS, BS), F32), ((ROWS, BS), F32), ((TERMS, BS), F32)),
            500,
            image, right_side, *c_sums, c_left, leaf_inverse, right, *mixes,
        )
        if step < ITERS - 1:
            terms = add_over(terms, FIRST)
            z_ring = [z] + ring(z.astype(BF))
            sums = siblings(add_over(terms, SECOND))
        else:
            sums = sibling_sums(*siblings(add_over(add_over(terms, FIRST), SECOND)))
            x = x + z - dot_t(left, sums)
    return x, resid


def solution(mesh):
    in_specs = (
        P(("drop", "blk"), None),
        P(("drop", "blk"), None, None, None),
        P(("drop", "blk"), None),
        P(("drop", "blk")),
        P(("drop", "blk"), None, None),
        P(None, None, ("drop", "blk")),
        P(None, None, ("drop", "blk")),
        P(None, None, ("drop", "blk")),
        P(None, None, ("drop", "blk")),
    )
    out_specs = (P(("drop", "blk"), None), P(("drop", "blk"), None))
    return jax.shard_map(on_device, mesh=mesh, in_specs=in_specs, out_specs=out_specs, check_vma=False)
```

```python
import functools

import jax
import jax.numpy as jnp
from jax import lax
from jax.experimental import pallas as pl
from jax.experimental.pallas import tpu as pltpu
from jax.sharding import PartitionSpec as P

ITERS = 3
AXES = ("drop", "blk")
BS = 128
NBD = 4
SLOTS = 40
R = 64
ROWS = NBD * BS
RING = 4 * ROWS
TERMS = 3 * R
PIECE = RING + TERMS
BF = jnp.bfloat16
F32 = jnp.float32


def coords(i):
    return i // 32, i // 16 % 2, i % 4, i // 4 % 4


def index(x, core, y, z):
    return (x % 4) * 32 + core * 16 + (z % 4) * 4 + y % 4


def pull(source):
    return [(source(i), i) for i in range(128)]


def along(axis, other):
    def source(i):
        x, core, y, z = coords(i)
        even = (x + core) % 2 == 1
        if even == (axis == 1):
            return index(x, core, other(y), z)
        return index(x, core, y, other(z))

    return pull(source)


FIRST = [along(1, lambda d, k=k: d + k) for k in (1, 3, 2)]
SECOND = [along(2, lambda d, k=k: d + k) for k in (1, 3, 2)]
CORE = pull(lambda i: i ^ 16)
CHIP = [pull(lambda i, k=k: i ^ (32 * k)) for k in (1, 2, 3)]


def groups_of_eight():
    out = []
    for p in range(4):
        for k in range(4):
            members = []
            for x, core in ((p, 1), (p + 1, 0)):
                for j in range(4):
                    members.append(index(x, core, k, j) if p % 2 == 0 else index(x, core, j, k))
            out.append(members)
    return out


EIGHTS = groups_of_eight()


def move(array, pairs):
    return lax.ppermute(array, AXES, pairs)


def ring(array):
    return [move(array, pairs) for pairs in FIRST]


def long_ring(array):
    half = array.shape[0] // 2
    up, down = move(array, FIRST[0]), move(array, FIRST[1])
    return [up, down, jnp.concatenate([move(up[:half], FIRST[0]), move(down[half:], FIRST[1])], axis=0)]


def add_over(term, steps):
    sent = term.astype(BF)
    return term + sum(move(sent, pairs).astype(F32) for pairs in steps)


def siblings(term, sent=None):
    other = move(term.astype(BF) if sent is None else sent, CORE)
    chip = term[R:] + other[R:].astype(F32)
    near = move(chip.astype(BF), CHIP[0])
    half = chip[R:] + near[R:].astype(F32)
    return other, near, move(half.astype(BF), CHIP[2])


def siblings_beside(other, term):
    chip = (term[R:] + other[R:].astype(F32)).astype(BF)
    return other, move(chip[:R], CHIP[0]), move(chip[R:], CHIP[1]), move(chip[R:], CHIP[2])


def sibling_sums(other, near, *far):
    last = far[0][...].astype(F32)
    for part in far[1:]:
        last = last + part[...].astype(F32)
    return jnp.concatenate([other[:R], near[:R], last.astype(BF)], axis=0)


def dot(a, b):
    return jnp.dot(a.astype(BF), b.astype(BF), preferred_element_type=F32)


def dot_t(a, b):
    return lax.dot_general(
        a.astype(BF), b.astype(BF), (((0,), (0,)), ((), ())), preferred_element_type=F32
    )


def dot_bt(a, b):
    return lax.dot_general(
        a.astype(BF), b.astype(BF), (((1,), (1,)), ((), ())), preferred_element_type=F32
    )


def slot_tables(neighbours, counts, half):
    drop, blk = lax.axis_index("drop"), lax.axis_index("blk")
    core, mine = drop % 2, (blk % 4, blk // 4)
    kind = neighbours // 64
    group = drop - 1 + kind
    block = neighbours % 64
    owner, part = block // 4, block % 4
    place = lax.rem(4 * kind + half + 8, 12) // 4
    even = (drop // 2 + core) % 2 == 1
    y_first = even == (place < 2)
    y, z = owner % 4, owner // 4
    first = jnp.where(y_first, y, z)
    second = jnp.where(y_first, z, y)
    mine_first = jnp.where(y_first, mine[0], mine[1])
    apart = (first - mine_first + 4) % 4
    at = jnp.where(apart < 2, apart, 5 - apart)
    member = jnp.where(place == 1, 4, 0) + second
    row = member * jnp.where(place < 2, PIECE, RING) + at * ROWS + part * BS
    slot = lax.broadcasted_iota(jnp.int32, neighbours.shape, 1)
    live = (slot < counts[:, None]) & (group >= 0) & (group <= 7)
    key = jnp.where(live, jnp.where(place < 2, 0, 1), 2)
    rank_key = key * SLOTS + slot
    rank = jnp.sum((rank_key[:, None, :] < rank_key[:, :, None]).astype(jnp.int32), axis=2)
    put = rank[:, :, None] == lax.broadcasted_iota(jnp.int32, (1, 1, SLOTS), 2)
    order = jnp.sum(jnp.where(put, slot[:, :, None], 0), axis=1)
    start = jnp.sum(jnp.where(put, jnp.where(live, row, 0)[:, :, None], 0), axis=1)
    n_pair = jnp.sum((key == 0).astype(jnp.int32), axis=1)
    n_live = jnp.sum((key < 2).astype(jnp.int32), axis=1)
    return order.reshape(-1), start.reshape(-1), n_pair, n_live


def near_kernel(width, order, start, lo, hi, blocks, field, before, out):
    rows = range(NBD)
    longest = hi[0] - lo[0]
    for q in rows[1:]:
        longest = jnp.maximum(longest, hi[q] - lo[q])

    def some(i, sums):
        new = []
        for q in rows:
            left, right = [], []
            for u in range(width):
                j = lo[q] + width * i + u
                at = q * SLOTS + jnp.minimum(j, SLOTS - 1)
                block = blocks[q, order[at]]
                left.append(jnp.where(j < hi[q], block, jnp.zeros_like(block)))
                row = jnp.minimum(start[at], field.shape[0] - BS)
                right.append(field[pl.ds(pl.multiple_of(row, 64), BS), :])
            new.append(
                sums[q]
                + jnp.dot(
                    jnp.concatenate(left, axis=1), jnp.concatenate(right, axis=0), preferred_element_type=F32
                )
            )
        return tuple(new)

    sums = tuple(before[q * BS : (q + 1) * BS, :] for q in rows)
    sums = lax.fori_loop(0, (longest + width - 1) // width, some, sums)
    for q in rows:
        out[q * BS : (q + 1) * BS, :] = sums[q]


def near(width, order, start, lo, hi, near_blocks, field, before):
    small, whole = pl.BlockSpec(memory_space=pltpu.SMEM), pl.BlockSpec(memory_space=pltpu.VMEM)
    return pl.pallas_call(
        functools.partial(near_kernel, width),
        in_specs=[small] * 4 + [whole] * 3,
        out_specs=whole,
        out_shape=jax.ShapeDtypeStruct((ROWS, BS), F32),
        compiler_params=pltpu.CompilerParams(vmem_limit_bytes=12 * 2**20),
        cost_estimate=pl.CostEstimate(flops=2 * 80 * BS**3, bytes_accessed=10 * 2**20, transcendentals=0),
    )(order, start, lo, hi, near_blocks, field, before)


def kernel_call(body, shapes, cost, *given):
    whole = pl.BlockSpec(memory_space=pltpu.VMEM)
    return pl.pallas_call(
        body,
        in_specs=[whole] * len(given),
        out_specs=[whole] * len(shapes),
        out_shape=[jax.ShapeDtypeStruct(*shape) for shape in shapes],
        compiler_params=pltpu.CompilerParams(vmem_limit_bytes=16 * 2**20),
        cost_estimate=pl.CostEstimate(flops=cost * 10**6, bytes_accessed=2**20, transcendentals=0),
    )(*given)


def start_kernel(has_field, *refs):
    *given, field, pieces = refs
    before, given = (given[0], given[1:]) if has_field else (None, given)
    z, up, down, far, other, near, last, *facts = given
    facts = facts[:4]
    sums = sibling_sums(other, near, last)
    c_terms = jnp.zeros((TERMS, BS), F32)
    for i, (part, fact) in enumerate(zip((z, up, down, far), facts)):
        rows = slice(i * ROWS, (i + 1) * ROWS)
        new = part[...].astype(F32) - dot_t(fact[:TERMS, :], sums)
        if has_field:
            new = before[rows, :] + new
        field[rows, :] = new
        new = new.astype(BF)
        for m in range(8):
            pieces[m, rows, :] = new
        c_terms = c_terms + dot(fact[TERMS:, :], new)
    c_terms = c_terms.astype(BF)
    for m in range(8):
        pieces[m, RING:, :] = c_terms


def sum_kernel(count, term, *refs):
    total = term[...]
    for part in refs[:count]:
        total = total + part[...].astype(F32)
    refs[-2][...] = total
    refs[-1][...] = total.astype(BF)


def finish_kernel(image, right_side, other, near, far_a, far_b, c_left, leaf_inverse, right, k10, k20, k21, resid, z, terms):
    sums = sibling_sums(other, near, far_a, far_b)
    left_over = right_side[...] - (image[...] + dot_t(c_left[...], sums))
    resid[...] = left_over
    left_over = left_over.astype(BF)
    for q in range(NBD):
        rows = slice(q * BS, (q + 1) * BS)
        z[rows, :] = dot(leaf_inverse[q], left_over[rows, :])
    terms[...] = fold(dot(right[...], z[...]), (k10[...], k20[...], k21[...]))


def leaf(resid, leaf_inverse):
    tiles = resid.astype(BF).reshape(NBD, BS, BS)
    return jnp.einsum("bij,bjn->bin", leaf_inverse, tiles, preferred_element_type=F32).reshape(ROWS, BS)


def first_terms(z, right, left):
    terms = dot(right, z)
    cross = dot_bt(right, left)
    low = jnp.concatenate([cross[R : 2 * R, :R], cross[2 * R :, :R]], axis=1)
    high = jnp.concatenate([cross[2 * R :, R : 2 * R]] * 2, axis=1)
    return jnp.concatenate([terms, low, high], axis=0)


def first_siblings(mine):
    other = move(mine.astype(BF), CORE).astype(F32)

    def parts(a):
        return a[:R], a[R : 2 * R], a[2 * R : 3 * R], a[3 * R : 4 * R, :R], a[3 * R : 4 * R, R:], a[4 * R :, :R]

    a0, a1, a2, m10, m20, m21 = parts(mine)
    b0, b1, b2, k10, k20, k21 = parts(other)
    t1 = a1 - dot(m10, b0) + b1 - dot(k10, a0)
    t2 = a2 - dot(m20, b0) + b2 - dot(k20, a0)
    m21 = m21 + k21
    chip = jnp.concatenate([t1, t2, jnp.concatenate([m21, m21], axis=1)], axis=0)
    near_chip = move(chip.astype(BF), CHIP[0]).astype(F32)
    s1, u2, k21 = near_chip[:R], near_chip[R : 2 * R], near_chip[2 * R :, :R]
    half = t2 - dot(m21, s1) + u2 - dot(k21, t1)
    s2 = move(half.astype(BF), CHIP[2])
    return (b0.astype(BF), s1.astype(BF), s2), (k10.astype(BF), k20.astype(BF), k21.astype(BF))


def fold(terms, mixes):
    k10, k20, k21 = mixes
    t0, t1, t2 = terms[:R], terms[R : 2 * R], terms[2 * R :]
    t1 = t1 - dot(k10, t0)
    t2 = t2 - dot(k20, t0) - dot(k21, t1)
    return jnp.concatenate([t0, t1, t2], axis=0)


def on_device(
    right_side, near_blocks, neighbours, counts, leaf_inverse, couple_left, couple_right, prec_left, prec_right
):
    half = 4 - 4 * (lax.axis_index("drop") % 2)
    order, start, n_pair, n_live = slot_tables(neighbours, counts, half)
    none = jnp.zeros_like(n_pair)
    c_left, c_right, left, right = (
        f.reshape(TERMS, ROWS) for f in (couple_left, couple_right, prec_left, prec_right)
    )

    facts = jnp.concatenate([left, c_right], axis=0)
    facts = [facts] + long_ring(facts)
    z = leaf(right_side, leaf_inverse)
    terms = first_terms(z, right, left)
    rest = ring(jnp.concatenate([z, terms], axis=0).astype(BF))
    terms = terms + sum(a[ROWS:].astype(F32) for a in rest)
    sums, mixes = first_siblings(add_over(terms, SECOND))
    field = None
    z_ring = [z] + [a[:ROWS] for a in rest]
    field_shape, piece_shape = ((RING, BS), F32), ((8, PIECE, BS), BF)

    for step in range(ITERS):
        given = [*z_ring, *sums, *facts]
        given = given + [order, start, n_pair, n_live] if step == 0 else [field] + given
        field, pieces = kernel_call(
            functools.partial(start_kernel, step > 0), (field_shape, piece_shape), 500, *given
        )
        pieces = lax.all_to_all(pieces, AXES, 0, 0, tiled=True, axis_index_groups=EIGHTS)
        c_parts = lax.dynamic_slice(pieces, (half, RING, 0), (4, TERMS, BS), allow_negative_indices=False)
        c_terms = jnp.sum(c_parts.astype(F32), axis=0)
        c_other = move(c_terms.astype(BF), CORE)
        pieces, c_other = lax.optimization_barrier((pieces, c_other))
        own = lax.dynamic_slice(pieces, (half, 0, 0), (4, RING, BS), allow_negative_indices=False)
        other = move(own, CORE)
        c_sums = siblings_beside(c_other, c_terms)
        x = field[:ROWS]
        image = near(8, order, start, none, n_pair, near_blocks, pieces.reshape(8 * PIECE, BS), x)
        image = near(8, order, start, n_pair, n_live, near_blocks, other.reshape(4 * RING, BS), image)
        resid, z, terms = kernel_call(
            finish_kernel,
            (((ROWS, BS), F32), ((ROWS, BS), F32), ((TERMS, BS), F32)),
            500,
            image, right_side, *c_sums, c_left, leaf_inverse, right, *mixes,
        )
        if step < ITERS - 1:
            terms = add_over(terms, FIRST)
            beside = ring(z.astype(BF))
            z_ring = [z] + beside
            term_b = terms.astype(BF)
            parts = [move(term_b, pairs) for pairs in SECOND]
            terms, term_b = kernel_call(
                functools.partial(sum_kernel, 3), (((TERMS, BS), F32), ((TERMS, BS), BF)), 1, terms, *parts, *beside[:2]
            )
            sums = siblings(terms, term_b)
        else:
            sums = sibling_sums(*siblings(add_over(add_over(terms, FIRST), SECOND)))
            x = x + z - dot_t(left, sums)
    return x, resid


def solution(mesh):
    in_specs = (
        P(("drop", "blk"), None),
        P(("drop", "blk"), None, None, None),
        P(("drop", "blk"), None),
        P(("drop", "blk")),
        P(("drop", "blk"), None, None),
        P(None, None, ("drop", "blk")),
        P(None, None, ("drop", "blk")),
        P(None, None, ("drop", "blk")),
        P(None, None, ("drop", "blk")),
    )
    out_specs = (P(("drop", "blk"), None), P(("drop", "blk"), None))
    return jax.shard_map(on_device, mesh=mesh, in_specs=in_specs, out_specs=out_specs, check_vma=False)
```

```python
import functools

import jax
import jax.numpy as jnp
from jax import lax
from jax.experimental import pallas as pl
from jax.experimental.pallas import tpu as pltpu
from jax.sharding import PartitionSpec as P

ITERS = 3
AXES = ("drop", "blk")
BS = 128
NBD = 4
SLOTS = 40
R = 64
ROWS = NBD * BS
RING = 4 * ROWS
TERMS = 3 * R
PIECE = RING + TERMS
BF = jnp.bfloat16
F32 = jnp.float32


def coords(i):
    return i // 32, i // 16 % 2, i % 4, i // 4 % 4


def index(x, core, y, z):
    return (x % 4) * 32 + core * 16 + (z % 4) * 4 + y % 4


def pull(source):
    return [(source(i), i) for i in range(128)]


def along(axis, other):
    def source(i):
        x, core, y, z = coords(i)
        even = (x + core) % 2 == 1
        if even == (axis == 1):
            return index(x, core, other(y), z)
        return index(x, core, y, other(z))

    return pull(source)


FIRST = [along(1, lambda d, k=k: d + k) for k in (1, 3, 2)]
SECOND = [along(2, lambda d, k=k: d + k) for k in (1, 3, 2)]
CORE = pull(lambda i: i ^ 16)
CHIP = [pull(lambda i, k=k: i ^ (32 * k)) for k in (1, 2, 3)]


def groups_of_eight():
    out = []
    for p in range(4):
        for k in range(4):
            members = []
            for x, core in ((p, 1), (p + 1, 0)):
                for j in range(4):
                    members.append(index(x, core, k, j) if p % 2 == 0 else index(x, core, j, k))
            out.append(members)
    return out


EIGHTS = groups_of_eight()


def move(array, pairs):
    return lax.ppermute(array, AXES, pairs)


def ring(array):
    return [move(array, pairs) for pairs in FIRST]


def long_ring(array):
    half = array.shape[0] // 2
    up, down = move(array, FIRST[0]), move(array, FIRST[1])
    return [up, down, jnp.concatenate([move(up[:half], FIRST[0]), move(down[half:], FIRST[1])], axis=0)]


def add_over(term, steps):
    sent = term.astype(BF)
    return term + sum(move(sent, pairs).astype(F32) for pairs in steps)


def siblings(term, sent=None):
    other = move(term.astype(BF) if sent is None else sent, CORE)
    chip = term[R:] + other[R:].astype(F32)
    near = move(chip.astype(BF), CHIP[0])
    half = chip[R:] + near[R:].astype(F32)
    return other, near, move(half.astype(BF), CHIP[2])


def siblings_beside(other, term):
    chip = (term[R:] + other[R:].astype(F32)).astype(BF)
    return other, move(chip[:R], CHIP[0]), move(chip[R:], CHIP[1]), move(chip[R:], CHIP[2])


def sibling_sums(other, near, *far):
    last = far[0][...].astype(F32)
    for part in far[1:]:
        last = last + part[...].astype(F32)
    return jnp.concatenate([other[:R], near[:R], last.astype(BF)], axis=0)


def dot(a, b):
    return jnp.dot(a.astype(BF), b.astype(BF), preferred_element_type=F32)


def dot_t(a, b):
    return lax.dot_general(
        a.astype(BF), b.astype(BF), (((0,), (0,)), ((), ())), preferred_element_type=F32
    )


def dot_bt(a, b):
    return lax.dot_general(
        a.astype(BF), b.astype(BF), (((1,), (1,)), ((), ())), preferred_element_type=F32
    )


def slot_tables(neighbours, counts, half):
    drop, blk = lax.axis_index("drop"), lax.axis_index("blk")
    core, mine = drop % 2, (blk % 4, blk // 4)
    kind = neighbours // 64
    group = drop - 1 + kind
    block = neighbours % 64
    owner, part = block // 4, block % 4
    place = lax.rem(4 * kind + half + 8, 12) // 4
    even = (drop // 2 + core) % 2 == 1
    y_first = even == (place < 2)
    y, z = owner % 4, owner // 4
    first = jnp.where(y_first, y, z)
    second = jnp.where(y_first, z, y)
    mine_first = jnp.where(y_first, mine[0], mine[1])
    apart = (first - mine_first + 4) % 4
    at = jnp.where(apart < 2, apart, 5 - apart)
    member = jnp.where(place == 1, 4, 0) + second
    row = member * jnp.where(place < 2, PIECE, RING) + at * ROWS + part * BS
    slot = lax.broadcasted_iota(jnp.int32, neighbours.shape, 1)
    live = (slot < counts[:, None]) & (group >= 0) & (group <= 7)
    key = jnp.where(live, jnp.where(place < 2, 0, 1), 2)
    rank_key = key * SLOTS + slot
    rank = jnp.sum((rank_key[:, None, :] < rank_key[:, :, None]).astype(jnp.int32), axis=2)
    put = rank[:, :, None] == lax.broadcasted_iota(jnp.int32, (1, 1, SLOTS), 2)
    order = jnp.sum(jnp.where(put, slot[:, :, None], 0), axis=1)
    start = jnp.sum(jnp.where(put, jnp.where(live, row, 0)[:, :, None], 0), axis=1)
    n_pair = jnp.sum((key == 0).astype(jnp.int32), axis=1)
    n_live = jnp.sum((key < 2).astype(jnp.int32), axis=1)
    return order.reshape(-1), start.reshape(-1), n_pair, n_live


def near_kernel(width, order, start, lo, hi, blocks, field, before, out):
    rows = range(NBD)
    longest = hi[0] - lo[0]
    for q in rows[1:]:
        longest = jnp.maximum(longest, hi[q] - lo[q])

    def some(i, sums):
        new = []
        for q in rows:
            left, right = [], []
            for u in range(width):
                j = lo[q] + width * i + u
                at = q * SLOTS + jnp.minimum(j, SLOTS - 1)
                block = blocks[q, order[at]]
                left.append(jnp.where(j < hi[q], block, jnp.zeros_like(block)))
                row = jnp.minimum(start[at], field.shape[0] - BS)
                right.append(field[pl.ds(pl.multiple_of(row, 64), BS), :])
            new.append(
                sums[q]
                + jnp.dot(
                    jnp.concatenate(left, axis=1), jnp.concatenate(right, axis=0), preferred_element_type=F32
                )
            )
        return tuple(new)

    sums = tuple(before[q * BS : (q + 1) * BS, :] for q in rows)
    sums = lax.fori_loop(0, (longest + width - 1) // width, some, sums)
    for q in rows:
        out[q * BS : (q + 1) * BS, :] = sums[q]


def near(width, order, start, lo, hi, near_blocks, field, before):
    small, whole = pl.BlockSpec(memory_space=pltpu.SMEM), pl.BlockSpec(memory_space=pltpu.VMEM)
    return pl.pallas_call(
        functools.partial(near_kernel, width),
        in_specs=[small] * 4 + [whole] * 3,
        out_specs=whole,
        out_shape=jax.ShapeDtypeStruct((ROWS, BS), F32),
        compiler_params=pltpu.CompilerParams(vmem_limit_bytes=12 * 2**20),
        cost_estimate=pl.CostEstimate(flops=2 * 80 * BS**3, bytes_accessed=10 * 2**20, transcendentals=0),
    )(order, start, lo, hi, near_blocks, field, before)


def kernel_call(body, shapes, cost, *given):
    whole = pl.BlockSpec(memory_space=pltpu.VMEM)
    return pl.pallas_call(
        body,
        in_specs=[whole] * len(given),
        out_specs=[whole] * len(shapes),
        out_shape=[jax.ShapeDtypeStruct(*shape) for shape in shapes],
        compiler_params=pltpu.CompilerParams(vmem_limit_bytes=16 * 2**20),
        cost_estimate=pl.CostEstimate(flops=cost * 10**6, bytes_accessed=2**20, transcendentals=0),
    )(*given)


def start_kernel(has_field, *refs):
    *given, field, pieces = refs
    before, given = (given[0], given[1:]) if has_field else (None, given)
    z, up, down, far, other, near, last, *facts = given
    facts = facts[:4]
    sums = sibling_sums(other, near, last)
    c_terms = jnp.zeros((TERMS, BS), F32)
    for i, (part, fact) in enumerate(zip((z, up, down, far), facts)):
        rows = slice(i * ROWS, (i + 1) * ROWS)
        new = part[...].astype(F32) - dot_t(fact[:TERMS, :], sums)
        if has_field:
            new = before[rows, :] + new
        field[rows, :] = new
        new = new.astype(BF)
        for m in range(8):
            pieces[m, rows, :] = new
        c_terms = c_terms + dot(fact[TERMS:, :], new)
    c_terms = c_terms.astype(BF)
    for m in range(8):
        pieces[m, RING:, :] = c_terms


def sum_kernel(count, term, *refs):
    total = term[...]
    for part in refs[:count]:
        total = total + part[...].astype(F32)
    refs[-2][...] = total
    refs[-1][...] = total.astype(BF)


def finish_kernel(image, right_side, other, near, far_a, far_b, c_left, leaf_inverse, right, k10, k20, k21, resid, z, terms):
    sums = sibling_sums(other, near, far_a, far_b)
    left_over = right_side[...] - (image[...] + dot_t(c_left[...], sums))
    resid[...] = left_over
    left_over = left_over.astype(BF)
    for q in range(NBD):
        rows = slice(q * BS, (q + 1) * BS)
        z[rows, :] = dot(leaf_inverse[q], left_over[rows, :])
    terms[...] = fold(dot(right[...], z[...]), (k10[...], k20[...], k21[...]))


def leaf(resid, leaf_inverse):
    tiles = resid.reshape(NBD, BS, BS)
    image = jnp.einsum("bij,bjn->bin", leaf_inverse.astype(F32), tiles, precision=lax.Precision.DEFAULT)
    return image.reshape(ROWS, BS)


def first_terms(z, right, left):
    terms = dot(right, z)
    cross = dot_bt(right, left)
    low = jnp.concatenate([cross[R : 2 * R, :R], cross[2 * R :, :R]], axis=1)
    high = jnp.concatenate([cross[2 * R :, R : 2 * R]] * 2, axis=1)
    return jnp.concatenate([terms, low, high], axis=0)


def first_siblings(mine):
    other = move(mine.astype(BF), CORE).astype(F32)

    def parts(a):
        return a[:R], a[R : 2 * R], a[2 * R : 3 * R], a[3 * R : 4 * R, :R], a[3 * R : 4 * R, R:], a[4 * R :, :R]

    a0, a1, a2, m10, m20, m21 = parts(mine)
    b0, b1, b2, k10, k20, k21 = parts(other)
    t1 = a1 - dot(m10, b0) + b1 - dot(k10, a0)
    t2 = a2 - dot(m20, b0) + b2 - dot(k20, a0)
    m21 = m21 + k21
    chip = jnp.concatenate([t1, t2, jnp.concatenate([m21, m21], axis=1)], axis=0)
    near_chip = move(chip.astype(BF), CHIP[0]).astype(F32)
    s1, u2, k21 = near_chip[:R], near_chip[R : 2 * R], near_chip[2 * R :, :R]
    half = t2 - dot(m21, s1) + u2 - dot(k21, t1)
    s2 = move(half.astype(BF), CHIP[2])
    return (b0.astype(BF), s1.astype(BF), s2), (k10.astype(BF), k20.astype(BF), k21.astype(BF))


def fold(terms, mixes):
    k10, k20, k21 = mixes
    t0, t1, t2 = terms[:R], terms[R : 2 * R], terms[2 * R :]
    t1 = t1 - dot(k10, t0)
    t2 = t2 - dot(k20, t0) - dot(k21, t1)
    return jnp.concatenate([t0, t1, t2], axis=0)


def on_device(
    right_side, near_blocks, neighbours, counts, leaf_inverse, couple_left, couple_right, prec_left, prec_right
):
    half = 4 - 4 * (lax.axis_index("drop") % 2)
    order, start, n_pair, n_live = slot_tables(neighbours, counts, half)
    none = jnp.zeros_like(n_pair)
    c_left, c_right, left, right = (
        f.reshape(TERMS, ROWS) for f in (couple_left, couple_right, prec_left, prec_right)
    )

    facts = jnp.concatenate([left, c_right], axis=0)
    facts = [facts] + long_ring(facts)
    z = leaf(right_side, leaf_inverse)
    terms = first_terms(z, right, left)
    rest = ring(jnp.concatenate([z, terms], axis=0).astype(BF))
    terms = terms + sum(a[ROWS:].astype(F32) for a in rest)
    sums, mixes = first_siblings(add_over(terms, SECOND))
    field = None
    z_ring = [z] + [a[:ROWS] for a in rest]
    field_shape, piece_shape = ((RING, BS), F32), ((8, PIECE, BS), BF)

    for step in range(ITERS):
        given = [*z_ring, *sums, *facts]
        given = given + [order, start, n_pair, n_live] if step == 0 else [field] + given
        field, pieces = kernel_call(
            functools.partial(start_kernel, step > 0), (field_shape, piece_shape), 500, *given
        )
        pieces = lax.all_to_all(pieces, AXES, 0, 0, tiled=True, axis_index_groups=EIGHTS)
        c_parts = lax.dynamic_slice(pieces, (half, RING, 0), (4, TERMS, BS), allow_negative_indices=False)
        c_terms = jnp.sum(c_parts.astype(F32), axis=0)
        c_other = move(c_terms.astype(BF), CORE)
        pieces, c_other = lax.optimization_barrier((pieces, c_other))
        own = lax.dynamic_slice(pieces, (half, 0, 0), (4, RING, BS), allow_negative_indices=False)
        other = move(own, CORE)
        c_sums = siblings_beside(c_other, c_terms)
        x = field[:ROWS]
        image = near(8, order, start, none, n_pair, near_blocks, pieces.reshape(8 * PIECE, BS), x)
        image = near(8, order, start, n_pair, n_live, near_blocks, other.reshape(4 * RING, BS), image)
        resid, z, terms = kernel_call(
            finish_kernel,
            (((ROWS, BS), F32), ((ROWS, BS), F32), ((TERMS, BS), F32)),
            500,
            image, right_side, *c_sums, c_left, leaf_inverse, right, *mixes,
        )
        if step < ITERS - 1:
            terms = add_over(terms, FIRST)
            beside = ring(z.astype(BF))
            z_ring = [z] + beside
            term_b = terms.astype(BF)
            parts = [move(term_b, pairs) for pairs in SECOND]
            terms, term_b = kernel_call(
                functools.partial(sum_kernel, 3), (((TERMS, BS), F32), ((TERMS, BS), BF)), 1, terms, *parts, *beside[:2]
            )
            sums = siblings(terms, term_b)
        else:
            sums = sibling_sums(*siblings(add_over(add_over(terms, FIRST), SECOND)))
            x = x + z - dot_t(left, sums)
    return x, resid


def solution(mesh):
    in_specs = (
        P(("drop", "blk"), None),
        P(("drop", "blk"), None, None, None),
        P(("drop", "blk"), None),
        P(("drop", "blk")),
        P(("drop", "blk"), None, None),
        P(None, None, ("drop", "blk")),
        P(None, None, ("drop", "blk")),
        P(None, None, ("drop", "blk")),
        P(None, None, ("drop", "blk")),
    )
    out_specs = (P(("drop", "blk"), None), P(("drop", "blk"), None))
    return jax.shard_map(on_device, mesh=mesh, in_specs=in_specs, out_specs=out_specs, check_vma=False)
```

```python
import functools

import jax
import jax.numpy as jnp
from jax import lax
from jax.experimental import pallas as pl
from jax.experimental.pallas import tpu as pltpu
from jax.sharding import PartitionSpec as P

ITERS = 3
AXES = ("drop", "blk")
BS = 128
NBD = 4
SLOTS = 40
R = 64
ROWS = NBD * BS
RING = 4 * ROWS
TERMS = 3 * R
PIECE = RING + TERMS
BF = jnp.bfloat16
F32 = jnp.float32


def coords(i):
    return i // 32, i // 16 % 2, i % 4, i // 4 % 4


def index(x, core, y, z):
    return (x % 4) * 32 + core * 16 + (z % 4) * 4 + y % 4


def pull(source):
    return [(source(i), i) for i in range(128)]


def along(axis, other):
    def source(i):
        x, core, y, z = coords(i)
        even = (x + core) % 2 == 1
        if even == (axis == 1):
            return index(x, core, other(y), z)
        return index(x, core, y, other(z))

    return pull(source)


FIRST = [along(1, lambda d, k=k: d + k) for k in (1, 3, 2)]
SECOND = [along(2, lambda d, k=k: d + k) for k in (1, 3, 2)]
CORE = pull(lambda i: i ^ 16)
CHIP = [pull(lambda i, k=k: i ^ (32 * k)) for k in (1, 2, 3)]


def groups_of_eight():
    out = []
    for p in range(4):
        for k in range(4):
            members = []
            for x, core in ((p, 1), (p + 1, 0)):
                for j in range(4):
                    members.append(index(x, core, k, j) if p % 2 == 0 else index(x, core, j, k))
            out.append(members)
    return out


EIGHTS = groups_of_eight()


def move(array, pairs):
    return lax.ppermute(array, AXES, pairs)


def ring(array):
    return [move(array, pairs) for pairs in FIRST]


def long_ring(array):
    half = array.shape[0] // 2
    up, down = move(array, FIRST[0]), move(array, FIRST[1])
    return [up, down, jnp.concatenate([move(up[:half], FIRST[0]), move(down[half:], FIRST[1])], axis=0)]


def add_over(term, steps):
    sent = term.astype(BF)
    return term + sum(move(sent, pairs).astype(F32) for pairs in steps)


def siblings(term, sent=None):
    other = move(term.astype(BF) if sent is None else sent, CORE)
    chip = term[R:] + other[R:].astype(F32)
    near = move(chip.astype(BF), CHIP[0])
    half = chip[R:] + near[R:].astype(F32)
    return other, near, move(half.astype(BF), CHIP[2])


def siblings_beside(other, term):
    chip = (term[R:] + other[R:].astype(F32)).astype(BF)
    return other, move(chip[:R], CHIP[0]), move(chip[R:], CHIP[1]), move(chip[R:], CHIP[2])


def sibling_sums(other, near, *far):
    last = far[0][...].astype(F32)
    for part in far[1:]:
        last = last + part[...].astype(F32)
    return jnp.concatenate([other[:R], near[:R], last.astype(BF)], axis=0)


def dot(a, b):
    return jnp.dot(a.astype(BF), b.astype(BF), preferred_element_type=F32)


def dot_t(a, b):
    return lax.dot_general(
        a.astype(BF), b.astype(BF), (((0,), (0,)), ((), ())), preferred_element_type=F32
    )


def dot_bt(a, b):
    return lax.dot_general(
        a.astype(BF), b.astype(BF), (((1,), (1,)), ((), ())), preferred_element_type=F32
    )


def slot_tables(neighbours, counts, half):
    drop, blk = lax.axis_index("drop"), lax.axis_index("blk")
    core, mine = drop % 2, (blk % 4, blk // 4)
    kind = neighbours // 64
    group = drop - 1 + kind
    block = neighbours % 64
    owner, part = block // 4, block % 4
    place = lax.rem(4 * kind + half + 8, 12) // 4
    even = (drop // 2 + core) % 2 == 1
    y_first = even == (place < 2)
    y, z = owner % 4, owner // 4
    first = jnp.where(y_first, y, z)
    second = jnp.where(y_first, z, y)
    mine_first = jnp.where(y_first, mine[0], mine[1])
    apart = (first - mine_first + 4) % 4
    at = jnp.where(apart < 2, apart, 5 - apart)
    member = jnp.where(place == 1, 4, 0) + second
    row = member * jnp.where(place < 2, PIECE, RING) + at * ROWS + part * BS
    slot = lax.broadcasted_iota(jnp.int32, neighbours.shape, 1)
    live = (slot < counts[:, None]) & (group >= 0) & (group <= 7)
    key = jnp.where(live, jnp.where(place < 2, 0, 1), 2)
    rank_key = key * SLOTS + slot
    rank = jnp.sum((rank_key[:, None, :] < rank_key[:, :, None]).astype(jnp.int32), axis=2)
    put = rank[:, :, None] == lax.broadcasted_iota(jnp.int32, (1, 1, SLOTS), 2)
    order = jnp.sum(jnp.where(put, slot[:, :, None], 0), axis=1)
    start = jnp.sum(jnp.where(put, jnp.where(live, row, 0)[:, :, None], 0), axis=1)
    n_pair = jnp.sum((key == 0).astype(jnp.int32), axis=1)
    n_live = jnp.sum((key < 2).astype(jnp.int32), axis=1)
    slots = order + start // 64 * 256
    return jnp.concatenate([slots.reshape(-1), jnp.zeros_like(n_pair), n_pair, n_live])


def near_kernel(part, width, table, blocks, field, before, out):
    rows = range(NBD)
    lo = [table[NBD * SLOTS + part * NBD + q] for q in rows]
    hi = [table[NBD * SLOTS + (part + 1) * NBD + q] for q in rows]
    longest = hi[0] - lo[0]
    for q in rows[1:]:
        longest = jnp.maximum(longest, hi[q] - lo[q])

    def some(i, sums):
        new = []
        for q in rows:
            left, right = [], []
            for u in range(width):
                j = lo[q] + width * i + u
                at = q * SLOTS + jnp.minimum(j, SLOTS - 1)
                slot = table[at]
                block = blocks[q, slot & 255]
                left.append(jnp.where(j < hi[q], block, jnp.zeros_like(block)))
                row = jnp.minimum((slot >> 8) * 64, field.shape[0] - BS)
                right.append(field[pl.ds(pl.multiple_of(row, 64), BS), :])
            new.append(
                sums[q]
                + jnp.dot(
                    jnp.concatenate(left, axis=1), jnp.concatenate(right, axis=0), preferred_element_type=F32
                )
            )
        return tuple(new)

    sums = tuple(before[q * BS : (q + 1) * BS, :] for q in rows)
    sums = lax.fori_loop(0, (longest + width - 1) // width, some, sums)
    for q in rows:
        out[q * BS : (q + 1) * BS, :] = sums[q]


def near(part, width, table, near_blocks, field, before):
    small, whole = pl.BlockSpec(memory_space=pltpu.SMEM), pl.BlockSpec(memory_space=pltpu.VMEM)
    return pl.pallas_call(
        functools.partial(near_kernel, part, width),
        in_specs=[small] + [whole] * 3,
        out_specs=whole,
        out_shape=jax.ShapeDtypeStruct((ROWS, BS), F32),
        compiler_params=pltpu.CompilerParams(vmem_limit_bytes=12 * 2**20),
        cost_estimate=pl.CostEstimate(flops=2 * 80 * BS**3, bytes_accessed=10 * 2**20, transcendentals=0),
    )(table, near_blocks, field, before)


def kernel_call(body, shapes, cost, *given):
    whole = pl.BlockSpec(memory_space=pltpu.VMEM)
    return pl.pallas_call(
        body,
        in_specs=[whole] * len(given),
        out_specs=[whole] * len(shapes),
        out_shape=[jax.ShapeDtypeStruct(*shape) for shape in shapes],
        compiler_params=pltpu.CompilerParams(vmem_limit_bytes=16 * 2**20),
        cost_estimate=pl.CostEstimate(flops=cost * 10**6, bytes_accessed=2**20, transcendentals=0),
    )(*given)


def start_kernel(has_field, *refs):
    *given, field, pieces = refs
    before, given = (given[0], given[1:]) if has_field else (None, given)
    z, up, down, far, other, near, last, *facts = given
    facts = facts[:4]
    sums = sibling_sums(other, near, last)
    c_terms = jnp.zeros((TERMS, BS), F32)
    for i, (part, fact) in enumerate(zip((z, up, down, far), facts)):
        rows = slice(i * ROWS, (i + 1) * ROWS)
        new = part[...].astype(F32) - dot_t(fact[:TERMS, :], sums)
        if has_field:
            new = before[rows, :] + new
        field[rows, :] = new
        new = new.astype(BF)
        for m in range(8):
            pieces[m, rows, :] = new
        c_terms = c_terms + dot(fact[TERMS:, :], new)
    c_terms = c_terms.astype(BF)
    for m in range(8):
        pieces[m, RING:, :] = c_terms


def sum_kernel(count, term, *refs):
    total = term[...]
    for part in refs[:count]:
        total = total + part[...].astype(F32)
    refs[-2][...] = total
    refs[-1][...] = total.astype(BF)


def finish_kernel(image, right_side, other, near, far_a, far_b, c_left, leaf_inverse, right, k10, k20, k21, z, terms, *resid):
    sums = sibling_sums(other, near, far_a, far_b)
    left_over = right_side[...] - (image[...] + dot_t(c_left[...], sums))
    for ref in resid:
        ref[...] = left_over
    left_over = left_over.astype(BF)
    for q in range(NBD):
        rows = slice(q * BS, (q + 1) * BS)
        z[rows, :] = dot(leaf_inverse[q], left_over[rows, :])
    terms[...] = fold(dot(right[...], z[...]), (k10[...], k20[...], k21[...]))


def leaf(resid, leaf_inverse):
    tiles = resid.reshape(NBD, BS, BS)
    image = jnp.einsum("bij,bjn->bin", leaf_inverse.astype(F32), tiles, precision=lax.Precision.DEFAULT)
    return image.reshape(ROWS, BS)


def first_terms(z, right, left):
    terms = dot(right, z)
    cross = dot_bt(right, left)
    low = jnp.concatenate([cross[R : 2 * R, :R], cross[2 * R :, :R]], axis=1)
    high = jnp.concatenate([cross[2 * R :, R : 2 * R]] * 2, axis=1)
    return jnp.concatenate([terms, low, high], axis=0)


def parts(a):
    return a[:R], a[R : 2 * R], a[2 * R : 3 * R], a[3 * R : 4 * R, :R], a[3 * R : 4 * R, R:], a[4 * R :, :R]


def first_chip_kernel(mine, other, chip, sent):
    a0, a1, a2, m10, m20, m21 = parts(mine[...])
    b0, b1, b2, k10, k20, k21 = parts(other[...].astype(F32))
    m21 = m21 + k21
    chip[:R, :] = a1 - dot(m10, b0) + b1 - dot(k10, a0)
    chip[R : 2 * R, :] = a2 - dot(m20, b0) + b2 - dot(k20, a0)
    chip[2 * R :, :] = jnp.concatenate([m21, m21], axis=1)
    sent[...] = chip[...].astype(BF)


def first_half_kernel(chip, near, sent):
    s1, u2, k21 = near[:R, :], near[R : 2 * R, :].astype(F32), near[2 * R :, :R]
    half = chip[R : 2 * R, :] - dot(chip[2 * R :, :R], s1) + u2 - dot(k21, chip[:R, :])
    sent[...] = half.astype(BF)


def first_siblings(mine):
    other = move(mine.astype(BF), CORE)
    chip, sent = kernel_call(first_chip_kernel, (((3 * R, BS), F32), ((3 * R, BS), BF)), 10, mine, other)
    near = move(sent, CHIP[0])
    (half,) = kernel_call(first_half_kernel, (((R, BS), BF),), 10, chip, near)
    b0, _, _, k10, k20, _ = parts(other)
    return (b0, near[:R], move(half, CHIP[2])), (k10, k20, near[2 * R :, :R])


def fold(terms, mixes):
    k10, k20, k21 = mixes
    t0, t1, t2 = terms[:R], terms[R : 2 * R], terms[2 * R :]
    t1 = t1 - dot(k10, t0)
    t2 = t2 - dot(k20, t0) - dot(k21, t1)
    return jnp.concatenate([t0, t1, t2], axis=0)


def on_device(
    right_side, near_blocks, neighbours, counts, leaf_inverse, couple_left, couple_right, prec_left, prec_right
):
    half = 4 - 4 * (lax.axis_index("drop") % 2)
    table = slot_tables(neighbours, counts, half)
    c_left, c_right, left, right = (
        f.reshape(TERMS, ROWS) for f in (couple_left, couple_right, prec_left, prec_right)
    )

    facts = jnp.concatenate([left, c_right], axis=0)
    facts = [facts] + long_ring(facts)
    z = leaf(right_side, leaf_inverse)
    terms = first_terms(z, right, left)
    rest = ring(jnp.concatenate([z, terms], axis=0).astype(BF))
    terms = terms + sum(a[ROWS:].astype(F32) for a in rest)
    sums, mixes = first_siblings(add_over(terms, SECOND))
    field = None
    z_ring = [z] + [a[:ROWS] for a in rest]
    field_shape, piece_shape = ((RING, BS), F32), ((8, PIECE, BS), BF)

    for step in range(ITERS):
        given = [*z_ring, *sums, *facts]
        given = given + [table] if step == 0 else [field] + given
        field, pieces = kernel_call(
            functools.partial(start_kernel, step > 0), (field_shape, piece_shape), 500, *given
        )
        pieces = lax.all_to_all(pieces, AXES, 0, 0, tiled=True, axis_index_groups=EIGHTS)
        c_parts = lax.dynamic_slice(pieces, (half, RING, 0), (4, TERMS, BS), allow_negative_indices=False)
        c_terms = jnp.sum(c_parts.astype(F32), axis=0)
        c_other = move(c_terms.astype(BF), CORE)
        pieces, c_other = lax.optimization_barrier((pieces, c_other))
        own = lax.dynamic_slice(pieces, (half, 0, 0), (4, RING, BS), allow_negative_indices=False)
        other = move(own, CORE)
        c_sums = siblings_beside(c_other, c_terms)
        x = field[:ROWS]
        image = near(0, 8, table, near_blocks, pieces.reshape(8 * PIECE, BS), x)
        image = near(1, 8, table, near_blocks, other.reshape(4 * RING, BS), image)
        shapes = (((ROWS, BS), F32), ((TERMS, BS), F32), ((ROWS, BS), F32))
        z, terms, *resid = kernel_call(
            finish_kernel,
            shapes if step == ITERS - 1 else shapes[:2],
            500,
            image, right_side, *c_sums, c_left, leaf_inverse, right, *mixes,
        )
        if step < ITERS - 1:
            terms = add_over(terms, FIRST)
            beside = ring(z.astype(BF))
            z_ring = [z] + beside
            term_b = terms.astype(BF)
            parts = [move(term_b, pairs) for pairs in SECOND]
            terms, term_b = kernel_call(
                functools.partial(sum_kernel, 3), (((TERMS, BS), F32), ((TERMS, BS), BF)), 1, terms, *parts, *beside[:2]
            )
            sums = siblings(terms, term_b)
        else:
            sums = sibling_sums(*siblings(add_over(add_over(terms, FIRST), SECOND)))
            x = x + z - dot_t(left, sums)
    return x, resid[0]


def solution(mesh):
    in_specs = (
        P(("drop", "blk"), None),
        P(("drop", "blk"), None, None, None),
        P(("drop", "blk"), None),
        P(("drop", "blk")),
        P(("drop", "blk"), None, None),
        P(None, None, ("drop", "blk")),
        P(None, None, ("drop", "blk")),
        P(None, None, ("drop", "blk")),
        P(None, None, ("drop", "blk")),
    )
    out_specs = (P(("drop", "blk"), None), P(("drop", "blk"), None))
    return jax.shard_map(on_device, mesh=mesh, in_specs=in_specs, out_specs=out_specs, check_vma=False)
```

```python
import functools

import jax
import jax.numpy as jnp
from jax import lax
from jax.experimental import pallas as pl
from jax.experimental.pallas import tpu as pltpu
from jax.sharding import PartitionSpec as P

ITERS = 3
AXES = ("drop", "blk")
BS = 128
NBD = 4
SLOTS = 40
R = 64
ROWS = NBD * BS
RING = 4 * ROWS
TERMS = 3 * R
PIECE = RING + TERMS
BF = jnp.bfloat16
F32 = jnp.float32


def coords(i):
    return i // 32, i // 16 % 2, i % 4, i // 4 % 4


def index(x, core, y, z):
    return (x % 4) * 32 + core * 16 + (z % 4) * 4 + y % 4


def pull(source):
    return [(source(i), i) for i in range(128)]


def along(axis, other):
    def source(i):
        x, core, y, z = coords(i)
        even = (x + core) % 2 == 1
        if even == (axis == 1):
            return index(x, core, other(y), z)
        return index(x, core, y, other(z))

    return pull(source)


FIRST = [along(1, lambda d, k=k: d + k) for k in (1, 3, 2)]
SECOND = [along(2, lambda d, k=k: d + k) for k in (1, 3, 2)]
CORE = pull(lambda i: i ^ 16)
CHIP = [pull(lambda i, k=k: i ^ (32 * k)) for k in (1, 2, 3)]


def groups_of_eight():
    out = []
    for p in range(4):
        for k in range(4):
            members = []
            for x, core in ((p, 1), (p + 1, 0)):
                for j in range(4):
                    members.append(index(x, core, k, j) if p % 2 == 0 else index(x, core, j, k))
            out.append(members)
    return out


EIGHTS = groups_of_eight()


def move(array, pairs):
    return lax.ppermute(array, AXES, pairs)


def ring(array):
    return [move(array, pairs) for pairs in FIRST]


def long_ring(array):
    half = array.shape[0] // 2
    up, down = move(array, FIRST[0]), move(array, FIRST[1])
    return [up, down, jnp.concatenate([move(up[:half], FIRST[0]), move(down[half:], FIRST[1])], axis=0)]


def add_over(term, steps):
    sent = term.astype(BF)
    return term + sum(move(sent, pairs).astype(F32) for pairs in steps)


def siblings(term, sent=None):
    other = move(term.astype(BF) if sent is None else sent, CORE)
    chip = term[R:] + other[R:].astype(F32)
    near = move(chip.astype(BF), CHIP[0])
    half = chip[R:] + near[R:].astype(F32)
    return other, near, move(half.astype(BF), CHIP[2])


def siblings_beside(other, term):
    chip = (term[R:] + other[R:].astype(F32)).astype(BF)
    return other, move(chip[:R], CHIP[0]), move(chip[R:], CHIP[1]), move(chip[R:], CHIP[2])


def sibling_sums(other, near, *far):
    last = far[0][...].astype(F32)
    for part in far[1:]:
        last = last + part[...].astype(F32)
    return jnp.concatenate([other[:R], near[:R], last.astype(BF)], axis=0)


def dot(a, b):
    return jnp.dot(a.astype(BF), b.astype(BF), preferred_element_type=F32)


def dot_t(a, b):
    return lax.dot_general(
        a.astype(BF), b.astype(BF), (((0,), (0,)), ((), ())), preferred_element_type=F32
    )


def dot_bt(a, b):
    return lax.dot_general(
        a.astype(BF), b.astype(BF), (((1,), (1,)), ((), ())), preferred_element_type=F32
    )


def slot_tables(neighbours, counts, half):
    drop, blk = lax.axis_index("drop"), lax.axis_index("blk")
    core, mine = drop % 2, (blk % 4, blk // 4)
    kind = neighbours // 64
    group = drop - 1 + kind
    block = neighbours % 64
    owner, part = block // 4, block % 4
    place = lax.rem(4 * kind + half + 8, 12) // 4
    even = (drop // 2 + core) % 2 == 1
    y_first = even == (place < 2)
    y, z = owner % 4, owner // 4
    first = jnp.where(y_first, y, z)
    second = jnp.where(y_first, z, y)
    mine_first = jnp.where(y_first, mine[0], mine[1])
    apart = (first - mine_first + 4) % 4
    at = jnp.where(apart < 2, apart, 5 - apart)
    member = jnp.where(place == 1, 4, 0) + second
    row = member * jnp.where(place < 2, PIECE, RING) + at * ROWS + part * BS
    slot = lax.broadcasted_iota(jnp.int32, neighbours.shape, 1)
    live = (slot < counts[:, None]) & (group >= 0) & (group <= 7)
    key = jnp.where(live, jnp.where(place < 2, 0, 1), 2)
    rank_key = key * SLOTS + slot
    rank = jnp.sum((rank_key[:, None, :] < rank_key[:, :, None]).astype(jnp.int32), axis=2)
    put = rank[:, :, None] == lax.broadcasted_iota(jnp.int32, (1, 1, SLOTS), 2)
    order = jnp.sum(jnp.where(put, slot[:, :, None], 0), axis=1)
    start = jnp.sum(jnp.where(put, jnp.where(live, row, 0)[:, :, None], 0), axis=1)
    n_pair = jnp.sum((key == 0).astype(jnp.int32), axis=1)
    n_live = jnp.sum((key < 2).astype(jnp.int32), axis=1)
    slots = order + start // 64 * 256
    return jnp.concatenate([slots.reshape(-1), jnp.zeros_like(n_pair), n_pair, n_live])


def near_kernel(part, width, table, blocks, field, before, out):
    rows = range(NBD)
    lo = [table[NBD * SLOTS + part * NBD + q] for q in rows]
    hi = [table[NBD * SLOTS + (part + 1) * NBD + q] for q in rows]
    longest = hi[0] - lo[0]
    for q in rows[1:]:
        longest = jnp.maximum(longest, hi[q] - lo[q])

    def some(i, sums):
        new = []
        for q in rows:
            left, right = [], []
            for u in range(width):
                j = lo[q] + width * i + u
                at = q * SLOTS + jnp.minimum(j, SLOTS - 1)
                slot = table[at]
                block = blocks[q, slot & 255]
                left.append(jnp.where(j < hi[q], block, jnp.zeros_like(block)))
                row = jnp.minimum((slot >> 8) * 64, field.shape[0] - BS)
                right.append(field[pl.ds(pl.multiple_of(row, 64), BS), :])
            new.append(
                sums[q]
                + jnp.dot(
                    jnp.concatenate(left, axis=1), jnp.concatenate(right, axis=0), preferred_element_type=F32
                )
            )
        return tuple(new)

    sums = tuple(before[q * BS : (q + 1) * BS, :] for q in rows)
    sums = lax.fori_loop(0, (longest + width - 1) // width, some, sums)
    for q in rows:
        out[q * BS : (q + 1) * BS, :] = sums[q]


def near(part, width, table, near_blocks, field, before):
    small, whole = pl.BlockSpec(memory_space=pltpu.SMEM), pl.BlockSpec(memory_space=pltpu.VMEM)
    return pl.pallas_call(
        functools.partial(near_kernel, part, width),
        in_specs=[small] + [whole] * 3,
        out_specs=whole,
        out_shape=jax.ShapeDtypeStruct((ROWS, BS), F32),
        compiler_params=pltpu.CompilerParams(vmem_limit_bytes=12 * 2**20),
        cost_estimate=pl.CostEstimate(flops=2 * 80 * BS**3, bytes_accessed=10 * 2**20, transcendentals=0),
    )(table, near_blocks, field, before)


def kernel_call(body, shapes, cost, *given):
    whole = pl.BlockSpec(memory_space=pltpu.VMEM)
    return pl.pallas_call(
        body,
        in_specs=[whole] * len(given),
        out_specs=[whole] * len(shapes),
        out_shape=[jax.ShapeDtypeStruct(*shape) for shape in shapes],
        compiler_params=pltpu.CompilerParams(vmem_limit_bytes=16 * 2**20),
        cost_estimate=pl.CostEstimate(flops=cost * 10**6, bytes_accessed=2**20, transcendentals=0),
    )(*given)


def start_kernel(has_field, *refs):
    *given, field, pieces = refs
    before, given = (given[0], given[1:]) if has_field else (None, given)
    z, up, down, far, other, near, last, *facts = given
    facts = facts[:4]
    sums = sibling_sums(other, near, last)
    c_terms = jnp.zeros((TERMS, BS), F32)
    for i, (part, fact) in enumerate(zip((z, up, down, far), facts)):
        rows = slice(i * ROWS, (i + 1) * ROWS)
        new = part[...].astype(F32) - dot_t(fact[:TERMS, :], sums)
        if has_field:
            new = before[rows, :] + new
        field[rows, :] = new
        new = new.astype(BF)
        for m in range(8):
            pieces[m, rows, :] = new
        c_terms = c_terms + dot(fact[TERMS:, :], new)
    c_terms = c_terms.astype(BF)
    for m in range(8):
        pieces[m, RING:, :] = c_terms


def sum_kernel(count, term, *refs):
    total = term[...]
    for part in refs[:count]:
        total = total + part[...].astype(F32)
    refs[-2][...] = total
    refs[-1][...] = total.astype(BF)


def finish_kernel(image, right_side, other, near, far_a, far_b, c_left, leaf_inverse, right, k10, k20, k21, resid, z, terms):
    sums = sibling_sums(other, near, far_a, far_b)
    left_over = right_side[...] - (image[...] + dot_t(c_left[...], sums))
    resid[...] = left_over
    left_over = left_over.astype(BF)
    for q in range(NBD):
        rows = slice(q * BS, (q + 1) * BS)
        z[rows, :] = dot(leaf_inverse[q], left_over[rows, :])
    terms[...] = fold(dot(right[...], z[...]), (k10[...], k20[...], k21[...]))


def leaf(resid, leaf_inverse):
    tiles = resid.reshape(NBD, BS, BS)
    image = jnp.einsum("bij,bjn->bin", leaf_inverse.astype(F32), tiles, precision=lax.Precision.DEFAULT)
    return image.reshape(ROWS, BS)


def first_terms(z, right, left):
    terms = dot(right, z)
    cross = dot_bt(right, left)
    low = jnp.concatenate([cross[R : 2 * R, :R], cross[2 * R :, :R]], axis=1)
    high = jnp.concatenate([cross[2 * R :, R : 2 * R]] * 2, axis=1)
    return jnp.concatenate([terms, low, high], axis=0)


def first_siblings(mine):
    other = move(mine.astype(BF), CORE).astype(F32)

    def parts(a):
        return a[:R], a[R : 2 * R], a[2 * R : 3 * R], a[3 * R : 4 * R, :R], a[3 * R : 4 * R, R:], a[4 * R :, :R]

    a0, a1, a2, m10, m20, m21 = parts(mine)
    b0, b1, b2, k10, k20, k21 = parts(other)
    t1 = a1 - dot(m10, b0) + b1 - dot(k10, a0)
    t2 = a2 - dot(m20, b0) + b2 - dot(k20, a0)
    m21 = m21 + k21
    chip = jnp.concatenate([t1, t2, jnp.concatenate([m21, m21], axis=1)], axis=0)
    near_chip = move(chip.astype(BF), CHIP[0]).astype(F32)
    s1, u2, k21 = near_chip[:R], near_chip[R : 2 * R], near_chip[2 * R :, :R]
    half = t2 - dot(m21, s1) + u2 - dot(k21, t1)
    s2 = move(half.astype(BF), CHIP[2])
    return (b0.astype(BF), s1.astype(BF), s2), (k10.astype(BF), k20.astype(BF), k21.astype(BF))


def fold(terms, mixes):
    k10, k20, k21 = mixes
    t0, t1, t2 = terms[:R], terms[R : 2 * R], terms[2 * R :]
    t1 = t1 - dot(k10, t0)
    t2 = t2 - dot(k20, t0) - dot(k21, t1)
    return jnp.concatenate([t0, t1, t2], axis=0)


def on_device(
    right_side, near_blocks, neighbours, counts, leaf_inverse, couple_left, couple_right, prec_left, prec_right
):
    half = 4 - 4 * (lax.axis_index("drop") % 2)
    table = slot_tables(neighbours, counts, half)
    c_left, c_right, left, right = (
        f.reshape(TERMS, ROWS) for f in (couple_left, couple_right, prec_left, prec_right)
    )

    facts = jnp.concatenate([left, c_right], axis=0)
    facts = [facts] + long_ring(facts)
    z = leaf(right_side, leaf_inverse)
    terms = first_terms(z, right, left)
    rest = ring(jnp.concatenate([z, terms], axis=0).astype(BF))
    terms = terms + sum(a[ROWS:].astype(F32) for a in rest)
    sums, mixes = first_siblings(add_over(terms, SECOND))
    field = None
    z_ring = [z] + [a[:ROWS] for a in rest]
    field_shape, piece_shape = ((RING, BS), F32), ((8, PIECE, BS), BF)

    for step in range(ITERS):
        given = [*z_ring, *sums, *facts]
        given = given + [table] if step == 0 else [field] + given
        field, pieces = kernel_call(
            functools.partial(start_kernel, step > 0), (field_shape, piece_shape), 500, *given
        )
        pieces = lax.all_to_all(pieces, AXES, 0, 0, tiled=True, axis_index_groups=EIGHTS)
        c_parts = lax.dynamic_slice(pieces, (half, RING, 0), (4, TERMS, BS), allow_negative_indices=False)
        c_terms = jnp.sum(c_parts.astype(F32), axis=0)
        c_other = move(c_terms.astype(BF), CORE)
        pieces, c_other = lax.optimization_barrier((pieces, c_other))
        own = lax.dynamic_slice(pieces, (half, 0, 0), (4, RING, BS), allow_negative_indices=False)
        other = move(own, CORE)
        c_sums = siblings_beside(c_other, c_terms)
        x = field[:ROWS]
        image = near(0, 8, table, near_blocks, pieces.reshape(8 * PIECE, BS), x)
        image = near(1, 8, table, near_blocks, other.reshape(4 * RING, BS), image)
        resid, z, terms = kernel_call(
            finish_kernel,
            (((ROWS, BS), F32), ((ROWS, BS), F32), ((TERMS, BS), F32)),
            500,
            image, right_side, *c_sums, c_left, leaf_inverse, right, *mixes,
        )
        if step < ITERS - 1:
            terms = add_over(terms, FIRST)
            beside = ring(z.astype(BF))
            z_ring = [z] + beside
            term_b = terms.astype(BF)
            parts = [move(term_b, pairs) for pairs in SECOND]
            terms, term_b = kernel_call(
                functools.partial(sum_kernel, 3), (((TERMS, BS), F32), ((TERMS, BS), BF)), 1, terms, *parts, *beside[:2]
            )
            sums = siblings(terms, term_b)
        else:
            sums = sibling_sums(*siblings(add_over(add_over(terms, FIRST), SECOND)))
            x = x + z - dot_t(left, sums)
    return x, resid


def solution(mesh):
    in_specs = (
        P(("drop", "blk"), None),
        P(("drop", "blk"), None, None, None),
        P(("drop", "blk"), None),
        P(("drop", "blk")),
        P(("drop", "blk"), None, None),
        P(None, None, ("drop", "blk")),
        P(None, None, ("drop", "blk")),
        P(None, None, ("drop", "blk")),
        P(None, None, ("drop", "blk")),
    )
    out_specs = (P(("drop", "blk"), None), P(("drop", "blk"), None))
    return jax.shard_map(on_device, mesh=mesh, in_specs=in_specs, out_specs=out_specs, check_vma=False)
```
